512 devices in a mesh: diam: 16 (over x, y_lo), mesh: 32 (over z, y_hi, core).
Axes of the slice: x: 4, y: 8 (y_hi: 2, y_lo: 4; y = y_hi * 4 + y_lo), z: 8, core: 2. Of those that a mesh axis runs over, the one named last changes fastest.
Arguments:
- perturbation: float32 [16, 2, 2, 5, 1024, 128], P('diam', None, None, None, 'mesh'), may hold values from -6 to 6
- source: float32 [2, 2, 5, 1024, 128], P(None, None, None, 'mesh'), may hold values from -6 to 6
- time_step: float32 [1024, 128], P('mesh'), may hold values from 0.25 to 0.3
- jac_axial: float32 [5, 5], replicated, may hold values from -3.354102 to 3.354102
- jac_circ: float32 [5, 5], replicated, may hold values from -3.354102 to 3.354102
- omega: float32 [2], replicated, may hold values from 0.5 to 2
- diam_ids: int32 [16], replicated, may hold values from 0 to 71, as said below
- surf_cell: int32 [16384], P('mesh'), may hold values from 0 to 4095
- surf_weight: float32 [16, 16384], P(None, 'mesh'), may hold values from -0.375 to 0.375
- face_count: int32 [32], P('mesh'), may hold values from 1 to 512, 8192 in all
Outputs:
- perturbation_new: float32 [16, 2, 2, 5, 1024, 128], P('diam', None, None, None, 'mesh')
- influence: float32 [16, 2, 2, 72], P('diam')
The draws below stay inside these ranges and needn't reach their ends.
Inputs may be any that keep to these rules, and one draw needn't show every extreme that they name: `diam_ids`: distinct nodal diameters; diameter 0 and diameter 72 - 1 are always among them. `face_count`: sum over blocks is 8192; some block owns all its 512 slots.
All inputs are finite; a program needn't handle non-finite values.
Results may differ from the reference program's by a relative error of at most 0.00017.
Values sent between devices are 32-bit elements; how exact they have to be, the bound alone decides.
No kernel may reach another device: no remote copies, remote signals or barrier semaphores. Data moves between devices by JAX's collectives and lax.ppermute only.
A program may use at most 64 MiB of HBM per device.

```python
import math
import jax
import jax.numpy as jnp
import numpy as np
from jax import lax

BLADES = 72
MODES = 16
EXC = 2
CI = 32
CJ = 128
FACE_DEV = 512
ITERS = 3
SECTIONS = 4
DIAMS = 16
NI = 1024
FACES = 16384
N_MESH = 32


def draw_diam_ids(key, part):
    key = jax.random.fold_in(key, 11)
    inner = jax.random.permutation(jax.random.fold_in(key, 1), BLADES - 2) + 1
    chosen = jnp.concatenate([jnp.array([0, BLADES - 1], dtype=jnp.int32), inner[:DIAMS - 2].astype(jnp.int32)])
    order = jax.random.permutation(jax.random.fold_in(key, 2), DIAMS)
    return chosen[order].astype(jnp.int32)


def place_ends(values, rng, least, largest):
    longest = values.shape.index(max(values.shape))
    spots = []
    for shift in (0, 1):
        where = [jax.random.randint(jax.random.fold_in(rng, axis), (), 0, length) for axis, length in enumerate(values.shape)]
        where[longest] = (where[longest] + shift) % values.shape[longest]
        spots.append(tuple(where))
    return values.at[spots[0]].set(least).at[spots[1]].set(largest)


def block_scale(own_key, shape, shards, smallest, largest):
    level, own = 1.0, jax.random.fold_in(own_key, 6)
    for dim, parts in shards:
        steps = jnp.exp(jax.random.uniform(jax.random.fold_in(own, dim), (parts,), jnp.float32, smallest / len(shards), largest / len(shards)))
        level = level * jnp.repeat(steps, shape[dim] // parts).reshape([-1 if axis == dim else 1 for axis in range(len(shape))])
    return level


def split_up(number_of, total, limit, skew):
    weights = [(1 << 20) // math.isqrt(standing ** skew) + 1 for standing in range(2, number_of + 1)]
    surplus, holding = total - limit - (number_of - 1), [1] * (number_of - 1)
    while surplus > 0:
        candidates = [i for i in range(number_of - 1) if holding[i] < limit]
        pool, remaining = sum([weights[i] for i in candidates]), surplus
        for i in candidates:
            more = min(limit - holding[i], max(1, remaining * weights[i] // pool), surplus)
            holding[i] = holding[i] + more
            surplus = surplus - more
    return np.array([limit] + holding)


def uneven_parts(key, amount, total, limit, skew):
    if amount == 2:
        one = jax.random.randint(key, (), max(1, total - limit), min(limit, total - 1) + 1)
        return jnp.stack([one, total - one])
    lengths = jnp.asarray(split_up(amount, total, limit, skew), jnp.int32)
    twos = (amount - 1) // 2
    source_of, receiver = lengths[1:1 + 2 * twos:2], lengths[2:2 + 2 * twos:2]
    room = jnp.minimum(source_of - 1, limit - receiver)
    passed = jax.random.randint(jax.random.fold_in(key, 1), (twos,), 0, 1 << 20) % (room + 1)
    lengths = lengths.at[1:1 + 2 * twos:2].set(source_of - passed).at[2:2 + 2 * twos:2].set(receiver + passed)
    return lengths[jax.random.permutation(jax.random.fold_in(key, 2), amount)]


def scatter_about(own_key, dims, deviation, reach, pieces=(), kind=jnp.bfloat16):
    loudness = block_scale(own_key, dims, pieces, -0.22, 0.18) if pieces else 1.0
    entries = jax.random.normal(own_key, dims, jnp.float32) * deviation * loudness
    return jnp.minimum(jnp.maximum(entries, -reach), reach).astype(kind)


def setup_inputs(seed: int = 0) -> dict:
    arg_keys = jax.random.split(jax.random.key(seed), 11)
    perturbation = scatter_about(arg_keys[0], (DIAMS, EXC, 2, 5, NI, CJ), 1.0, 6.0, ((0, 16), (4, 32)), jnp.float32)
    source = scatter_about(arg_keys[1], (EXC, 2, 5, NI, CJ), 1.0, 6.0, ((3, 32),), jnp.float32)
    time_step = jnp.clip(0.25 + 0.050000012 * jax.random.uniform(arg_keys[2], (NI, CJ), jnp.float32) ** block_scale(arg_keys[2], (NI, CJ), ((0, 32),), -0.2, 0.2), 0.25, 0.3)
    jac_axial = scatter_about(arg_keys[3], (5, 5), (3.0 / 5 ** 0.5), 3.354102, (), jnp.float32)
    jac_circ = scatter_about(arg_keys[4], (5, 5), (3.0 / 5 ** 0.5), 3.354102, (), jnp.float32)
    omega = jnp.clip(jnp.exp(jax.random.uniform(arg_keys[5], (EXC,), jnp.float32, math.log(0.5), math.log(2.0))), 0.5, 2.0)
    diam_ids = draw_diam_ids(jax.random.fold_in(arg_keys[10], 71), 0)
    surf_cell = place_ends(jax.random.randint(arg_keys[7], (FACES,), 0, CI * CJ), jax.random.fold_in(arg_keys[7], 1), 0, (CI * CJ) - 1).astype(jnp.int32)
    surf_weight = scatter_about(arg_keys[8], (MODES, FACES), (8.0 / (FACES ** 0.5)), 0.375, ((1, 32),), jnp.float32)
    face_count = uneven_parts(arg_keys[9], N_MESH, FACES // 2, FACE_DEV, 2).astype(jnp.int32)
    return dict(perturbation=perturbation, source=source, time_step=time_step, jac_axial=jac_axial, jac_circ=jac_circ, omega=omega, diam_ids=diam_ids, surf_cell=surf_cell, surf_weight=surf_weight, face_count=face_count)


HIGH = lax.Precision.HIGHEST
ALPHAS = (0.25, 1.0 / 3.0, 0.5, 1.0)


def rotate(field, cosine, sine):
    real_part = field[:, :, 0:1]
    imag_part = field[:, :, 1:2]
    return jnp.concatenate([cosine * real_part - sine * imag_part, sine * real_part + cosine * imag_part], axis=2)


def rhs(center, upper, lower, cosine, sine, src, jac_axial, jac_circ, omega):
    width = center.shape[-1]
    column = jnp.arange(width)
    right_base = jnp.roll(center, -1, axis=-1)
    right = jnp.where(column == width - 1, rotate(right_base, cosine, sine), right_base)
    left_base = jnp.roll(center, 1, axis=-1)
    left = jnp.where(column == 0, rotate(left_base, cosine, -sine), left_base)
    axial = (upper - lower) * 0.5
    circ = (right - left) * 0.5
    lap = upper + lower + right + left - 4.0 * center
    conv = jnp.einsum("uv,decvij->decuij", jac_axial, axial, precision=HIGH)
    conv = conv + jnp.einsum("uv,decvij->decuij", jac_circ, circ, precision=HIGH)
    freq = omega.reshape(1, -1, 1, 1, 1, 1)
    spin = jnp.concatenate([-freq * center[:, :, 1:2], freq * center[:, :, 0:1]], axis=2)
    return spin + conv - 0.2 * lap - src[None]


def sweep_slot(args):
    field, ident, source, time_step, jac_axial, jac_circ, omega = args
    sigma = 2.0 * jnp.pi * ident.astype(jnp.float32) / BLADES
    cosine = jnp.cos(sigma)
    sine = jnp.sin(sigma)
    q = field[None]
    for step in range(ITERS):
        q0 = q
        for section in range(SECTIONS):
            padded = jnp.pad(q, ((0, 0), (0, 0), (0, 0), (0, 0), (1, 1), (0, 0)))
            res = rhs(q, padded[..., 2:, :], padded[..., :-2, :], cosine, sine, source, jac_axial, jac_circ, omega)
            q = q0 - ALPHAS[section] * time_step * res
    return q[0]


def reference(perturbation, source, time_step, jac_axial, jac_circ, omega, diam_ids, surf_cell, surf_weight, face_count):
    def one(pair):
        return sweep_slot((pair[0], pair[1], source, time_step, jac_axial, jac_circ, omega))

    result = lax.map(one, (perturbation, diam_ids))
    block = jnp.arange(FACES, dtype=jnp.int32) // FACE_DEV
    slot = jnp.arange(FACES, dtype=jnp.int32) % FACE_DEV
    live = (slot < face_count[block]).astype(jnp.float32)
    where_cell = block * (CI * CJ) + surf_cell
    pressure = result[:, :, :, 4].reshape(DIAMS, EXC, 2, NI * CJ)
    picked = jnp.take(pressure, where_cell, axis=3) * live
    force = jnp.einsum("decf,mf->decm", picked, surf_weight, precision=HIGH)
    blade = jnp.arange(BLADES, dtype=jnp.int32)
    angle = 2.0 * jnp.pi * ((diam_ids[:, None] * blade[None, :]) % BLADES).astype(jnp.float32) / BLADES
    cosine = jnp.cos(angle)
    sine = jnp.sin(angle)
    f_real = force[:, :, 0]
    f_imag = force[:, :, 1]
    k_real = jnp.einsum("nem,nb->meb", f_real, cosine, precision=HIGH) - jnp.einsum("nem,nb->meb", f_imag, sine, precision=HIGH)
    k_imag = jnp.einsum("nem,nb->meb", f_real, sine, precision=HIGH) + jnp.einsum("nem,nb->meb", f_imag, cosine, precision=HIGH)
    influence = jnp.stack([k_real, k_imag], axis=1) / BLADES
    return result, influence
```

```python
import functools
import itertools

import jax
import jax.numpy as jnp
from jax import lax
from jax.experimental import pallas as pl
from jax.experimental.pallas import tpu as pltpu
from jax.sharding import Mesh
from jax.sharding import PartitionSpec as P

BLADES = 72
ITERS = 3
SECTIONS = 4
HALO = ITERS * SECTIONS
ALPHAS = (0.25, 1.0 / 3.0, 0.5, 1.0)
HIGH = lax.Precision.HIGHEST
AXES = ("x", "yl", "z", "yh", "core")
SIZES = (4, 4, 8, 2, 2)
PLANES = 20
ROWS = 32
LANES = 128
MSG = 2 * PLANES * HALO + 16
TOP = 8
OWN = TOP + HALO
LOW = OWN + ROWS
BUF = LOW + HALO + 8


def flat(*coords):
    out = 0
    for c, n in zip(coords, SIZES):
        out = out * n + c
    return out


def swap_pairs(same_chip):
    pairs = []
    blocks = SIZES[2] * SIZES[3] * SIZES[4]
    for x, yl, p in itertools.product(range(SIZES[0]), range(SIZES[1]), range(blocks)):
        if same_chip:
            q = p ^ 1
        else:
            q = p + 1 if p % 2 else p - 1
        if 0 <= q < blocks:
            ends = [flat(x, yl, b // 4, (b // 2) % 2, b % 2) for b in (p, q)]
            pairs.append(tuple(ends))
    return pairs


def pack_kernel(q_ref, s_ref, t_ref, near_ref, far_ref):
    even = lax.axis_index("core") == 0

    def put(row, low, high):
        near_ref[pl.ds(row, HALO), :] = jnp.where(even, high, low)
        far_ref[pl.ds(row, HALO), :] = jnp.where(even, low, high)

    for i in range(PLANES):
        put(i * HALO, q_ref[i, 0:HALO, :], q_ref[i, ROWS - HALO : ROWS, :])
        put((PLANES + i) * HALO, s_ref[i, 0:HALO, :], s_ref[i, ROWS - HALO : ROWS, :])
    put(2 * PLANES * HALO, t_ref[0:HALO, :], t_ref[ROWS - HALO : ROWS, :])
    tail = jnp.zeros((MSG - 2 * PLANES * HALO - HALO, LANES), jnp.float32)
    near_ref[MSG - tail.shape[0] :, :] = tail
    far_ref[MSG - tail.shape[0] :, :] = tail


def prep_kernel(cell_ref, weight_ref, count_ref, ids_ref, moments_ref, table_ref):
    faces = cell_ref.shape[1]
    modes = weight_ref.shape[0]
    cell = cell_ref[...]
    row = lax.shift_right_logical(cell, 7)
    col = jnp.bitwise_and(cell, LANES - 1)
    live = lax.broadcasted_iota(jnp.int32, (1, faces), 1) < count_ref[0]
    weight = jnp.where(live, weight_ref[...], 0.0)
    in_row = lax.broadcasted_iota(jnp.int32, (ROWS, faces), 0) == row
    in_col = (lax.broadcasted_iota(jnp.int32, (LANES, faces), 0) == col).astype(jnp.float32)
    spread = jnp.concatenate(
        [jnp.where(in_row, weight[m : m + 1, :], 0.0) for m in range(modes)], axis=0
    )
    moments_ref[...] = lax.dot_general(
        spread, in_col, (((1,), (1,)), ((), ())), precision=HIGH, preferred_element_type=jnp.float32
    )

    blade = lax.broadcasted_iota(jnp.int32, (1, LANES), 1)
    rows = []
    for yl, x in itertools.product(range(SIZES[1]), range(SIZES[0])):
        rows.append(blade * ids_ref[x * SIZES[1] + yl])
    product = jnp.concatenate(rows, axis=0)
    turns = ((product.astype(jnp.float32) + 0.5) * (1.0 / BLADES)).astype(jnp.int32)
    angle = 2.0 * jnp.pi * (product - turns * BLADES).astype(jnp.float32) / BLADES
    n = len(rows)
    table_ref[0:n, :] = jnp.cos(angle)
    table_ref[n : 2 * n, :] = jnp.sin(angle)
    mine = ids_ref[lax.axis_index("x") * SIZES[1] + lax.axis_index("yl")]
    sigma = jnp.full((8, LANES), mine, jnp.int32).astype(jnp.float32)
    sigma = 2.0 * jnp.pi * sigma / BLADES
    table_ref[2 * n : 2 * n + 8, :] = jnp.cos(sigma)
    table_ref[2 * n + 8 : 2 * n + 16, :] = jnp.sin(sigma)


def sweep_kernel(
    ja_ref, jc_ref, omega_ref, q_ref, s_ref, t_ref, near_ref, far_ref, moments_ref, table_ref,
    out_ref, force_ref, base, first, second, forced, step,
):
    even = lax.axis_index("core") == 0
    edge = jnp.zeros((8, LANES), jnp.float32)
    for buf in (base, first, second):
        for i in range(PLANES):
            buf[i, 0:8, :] = edge
            buf[i, BUF - 8 : BUF, :] = edge

    def put(buf, row, own):
        near = near_ref[pl.ds(row, HALO), :]
        far = far_ref[pl.ds(row, HALO), :]
        buf[TOP:OWN, :] = jnp.where(even, far, near)
        buf[OWN:LOW, :] = own
        buf[LOW : LOW + HALO, :] = jnp.where(even, near, far)

    for i in range(PLANES):
        put(base.at[i], i * HALO, q_ref[i])
        put(forced.at[i], (PLANES + i) * HALO, s_ref[i])
    put(step, 2 * PLANES * HALO, t_ref[...])

    lane = lax.broadcasted_iota(jnp.int32, (8, LANES), 1)
    is_first, is_last = lane == 0, lane == LANES - 1
    cosine = table_ref[32:40, :]
    sine = table_ref[40:48, :]
    turn_c = jnp.where(is_first | is_last, cosine, 1.0)
    turn_s = jnp.where(is_first, -sine, jnp.where(is_last, sine, 0.0))

    def section(cur, new, alpha, row):
        here = pl.ds(row, 8)
        dt = step[here, :] * alpha
        for e in range(2):
            center, axial, circ, total = [], [], [], []
            for c in range(2):
                for v in range(5):
                    i = e * 10 + c * 5 + v
                    center.append(cur[i, here, :])
            for c in range(2):
                for v in range(5):
                    i = e * 10 + c * 5 + v
                    up = cur[i, pl.ds(row + 1, 8), :]
                    down = cur[i, pl.ds(row - 1, 8), :]
                    mid, other = center[c * 5 + v], center[(1 - c) * 5 + v]
                    if c == 0:
                        turned = turn_c * mid + turn_s * other
                    else:
                        turned = turn_c * mid - turn_s * other
                    right = pltpu.roll(jnp.where(is_first, turned, mid), LANES - 1, 1)
                    left = pltpu.roll(jnp.where(is_last, turned, mid), 1, 1)
                    axial.append(up - down)
                    circ.append(right - left)
                    total.append((up + down) + (right + left))
            freq = omega_ref[e]
            for c in range(2):
                for u in range(5):
                    i = e * 10 + c * 5 + u
                    conv = None
                    for v in range(5):
                        a = (ja_ref[u, v] * 0.5) * axial[c * 5 + v]
                        b = (jc_ref[u, v] * 0.5) * circ[c * 5 + v]
                        conv = a + b if conv is None else conv + (a + b)
                    spin = freq * center[(1 - c) * 5 + u]
                    res = conv - 0.2 * total[c * 5 + u] + 0.8 * center[c * 5 + u] - forced[i, here, :]
                    res = res - spin if c == 0 else res + spin
                    new[i, here, :] = base[i, here, :] - dt * res

    bufs = (base, first, second, first, base)
    for it in range(ITERS):
        for k in range(SECTIONS):
            reach = HALO - 1 - (it * SECTIONS + k)
            start = OWN - reach
            tiles = (ROWS + 2 * reach + 7) // 8

            def body(j, carry, cur=bufs[k], new=bufs[k + 1], alpha=ALPHAS[k], start=start):
                section(cur, new, alpha, start + j * 8)
                return carry

            lax.fori_loop(0, tiles, body, 0)

    for i in range(PLANES):
        out_ref[i] = base[i, OWN:LOW, :]

    sums = []
    modes = moments_ref.shape[0] // ROWS
    for m in range(modes):
        for ec in range(4):
            acc = None
            for r in range(0, ROWS, 8):
                term = moments_ref[m * ROWS + r : m * ROWS + r + 8, :] * base[ec * 5 + 4, OWN + r : OWN + r + 8, :]
                acc = term if acc is None else acc + term
            sums.append(acc)
    stacked = jnp.concatenate(sums, axis=0)
    count = len(sums)
    pick = lax.broadcasted_iota(jnp.int32, (LANES, count * 8), 1) // 8
    pick = (pick == lax.broadcasted_iota(jnp.int32, (LANES, count * 8), 0)).astype(jnp.float32)
    by_lane = jnp.dot(pick, stacked, precision=HIGH, preferred_element_type=jnp.float32)
    ones = jnp.ones(force_ref.shape, jnp.float32)
    force_ref[...] = lax.dot_general(
        ones, by_lane, (((1,), (1,)), ((), ())), precision=HIGH, preferred_element_type=jnp.float32
    )


def middle_kernel(in_ref, out_ref):
    got = in_ref[...]
    mine = lax.axis_index("yl")
    lane = lax.broadcasted_iota(jnp.int32, (1, LANES), 1)
    keep = (lane % 16 < 4) & (lane < 64)
    total = None
    for yl in range(SIZES[1]):
        part = jnp.sum(got[yl * 4 : yl * 4 + 4, :], axis=0, keepdims=True)
        part = pltpu.roll(part, (LANES - 4 * mine) % LANES, 1)
        part = jnp.where(keep, part, 0.0)
        if yl:
            part = pltpu.roll(part, 4 * yl, 1)
        total = part if total is None else total + part
    out_ref[...] = jnp.broadcast_to(total, out_ref.shape)


def final_kernel(in_ref, table_ref, out_ref):
    mine = lax.axis_index("x")
    depth = SIZES[2]
    parts = [
        jnp.sum(in_ref[x * depth : (x + 1) * depth, :], axis=0, keepdims=True) for x in range(SIZES[0])
    ]
    force = pltpu.roll(jnp.concatenate(parts, axis=0), (LANES - 16 * mine) % LANES, 1)
    n = SIZES[0] * SIZES[1]
    for e in range(2):
        real, imag = None, None
        for yl in range(SIZES[1]):
            at = yl * 4 + e * 2
            f_r = force[:, at : at + 1]
            f_i = force[:, at + 1 : at + 2]
            cosine = table_ref[yl * 4 : yl * 4 + 4, :]
            sine = table_ref[n + yl * 4 : n + yl * 4 + 4, :]
            r = f_r * cosine - f_i * sine
            i = f_r * sine + f_i * cosine
            real = r if real is None else real + r
            imag = i if imag is None else imag + i
        scale = 1.0 / BLADES
        out_ref[0, 0, e : e + 1, :] = (jnp.sum(real, axis=0, keepdims=True) * scale)[:, :BLADES]
        out_ref[0, 1, e : e + 1, :] = (jnp.sum(imag, axis=0, keepdims=True) * scale)[:, :BLADES]


def shape(*dims):
    return jax.ShapeDtypeStruct(dims, jnp.float32)


VMEM = pl.BlockSpec(memory_space=pltpu.VMEM)
SMEM = pl.BlockSpec(memory_space=pltpu.SMEM)


def call(kernel, out_shape, in_specs, scratch=(), cost=(1000, 1000)):
    return pl.pallas_call(
        kernel,
        out_shape=out_shape,
        in_specs=in_specs,
        out_specs=jax.tree.map(lambda _: VMEM, out_shape),
        scratch_shapes=list(scratch),
        compiler_params=pltpu.CompilerParams(vmem_limit_bytes=32 * 1024 * 1024),
        cost_estimate=pl.CostEstimate(flops=cost[0], bytes_accessed=cost[1], transcendentals=0),
    )


def per_device(
    perturbation, source, time_step, jac_axial, jac_circ, omega, diam_ids, surf_cell, surf_weight, face_count
):
    q = perturbation.reshape(PLANES, ROWS, LANES)
    src = source.reshape(PLANES, ROWS, LANES)
    near, far = call(pack_kernel, (shape(MSG, LANES),) * 2, [VMEM] * 3)(q, src, time_step)
    far = lax.ppermute(far, AXES, swap_pairs(False))
    near = lax.ppermute(near, AXES, swap_pairs(True))
    moments, table = call(
        prep_kernel, (shape(16 * ROWS, LANES), shape(48, LANES)), [VMEM, VMEM, SMEM, SMEM], cost=(400_000_000, 1_000_000)
    )(surf_cell.reshape(1, -1), surf_weight, face_count, diam_ids)
    big = pltpu.VMEM((PLANES, BUF, LANES), jnp.float32)
    result, force = call(
        sweep_kernel,
        (shape(PLANES, ROWS, LANES), shape(16, LANES)),
        [SMEM] * 3 + [VMEM] * 7,
        [big, big, big, big, pltpu.VMEM((BUF, LANES), jnp.float32)],
        cost=(100_000_000, 2_000_000),
    )(jac_axial, jac_circ, omega, q, src, time_step, near, far, moments, table)
    got = lax.all_to_all(force, ("yl", "yh", "core"), 0, 0, tiled=True)
    middle = call(middle_kernel, shape(32, LANES), [VMEM])(got)
    got = lax.all_to_all(middle, ("x", "z"), 0, 0, tiled=True)
    influence = call(final_kernel, shape(1, 2, 2, BLADES), [VMEM, VMEM])(got, table)
    return result.reshape(perturbation.shape), influence


def solution(mesh):
    fine = Mesh(mesh.devices.reshape(SIZES), AXES)
    diam, blocks = ("x", "yl"), ("z", "yh", "core")
    in_specs = (
        P(diam, None, None, None, blocks, None),
        P(None, None, None, blocks, None),
        P(blocks, None),
        P(),
        P(),
        P(),
        P(),
        P(blocks),
        P(None, blocks),
        P(blocks),
    )
    out_specs = (P(diam, None, None, None, blocks, None), P(diam, None, None, None))
    return jax.shard_map(per_device, mesh=fine, in_specs=in_specs, out_specs=out_specs, check_vma=False)
```

```python
import itertools

import jax
import jax.numpy as jnp
from jax import lax
from jax.experimental import pallas as pl
from jax.experimental.pallas import tpu as pltpu
from jax.sharding import Mesh
from jax.sharding import PartitionSpec as P

BLADES = 72
ITERS = 3
SECTIONS = 4
HALO = ITERS * SECTIONS
ALPHAS = (0.25, 1.0 / 3.0, 0.5, 1.0)
HIGH = lax.Precision.HIGHEST
AXES = ("x", "yl", "z", "yh", "core")
SIZES = (4, 4, 8, 2, 2)
PLANES = 20
ROWS = 32
LANES = 128
MSG = 2 * PLANES * HALO + 16
LEVELS = HALO
OWN = 8
PART = 32
TILE = 8


def flat(*coords):
    out = 0
    for c, n in zip(coords, SIZES):
        out = out * n + c
    return out


def swap_pairs(same_chip):
    pairs = []
    blocks = SIZES[2] * SIZES[3] * SIZES[4]
    for x, yl, p in itertools.product(range(SIZES[0]), range(SIZES[1]), range(blocks)):
        if same_chip:
            q = p ^ 1
        else:
            q = p + 1 if p % 2 else p - 1
        if 0 <= q < blocks:
            ends = [flat(x, yl, b // 4, (b // 2) % 2, b % 2) for b in (p, q)]
            pairs.append(tuple(ends))
    return pairs


def pack_kernel(q_ref, s_ref, t_ref, near_ref, far_ref, q_buf, s_buf, t_buf, sems):
    core = lax.axis_index("core")
    wide = q_buf.shape[2]
    copies = []
    for side in range(2):
        start = (core if side == 0 else 1 - core) * (ROWS - wide)
        rows = pl.ds(pl.multiple_of(start, TILE), wide)
        copies.append(pltpu.make_async_copy(q_ref.at[:, rows, :], q_buf.at[side], sems.at[side, 0]))
        copies.append(pltpu.make_async_copy(s_ref.at[:, rows, :], s_buf.at[side], sems.at[side, 1]))
        copies.append(pltpu.make_async_copy(t_ref.at[rows, :], t_buf.at[side], sems.at[side, 2]))
    for copy in copies:
        copy.start()
    for side, out in ((0, far_ref), (1, near_ref)):
        for copy in copies[side * 3 : side * 3 + 3]:
            copy.wait()
        shift = (core if side == 0 else 1 - core) * (wide - HALO)
        rows = pl.ds(shift, HALO)
        for i in range(PLANES):
            out[i * HALO : (i + 1) * HALO, :] = q_buf[side, i, rows, :]
            out[(PLANES + i) * HALO : (PLANES + i + 1) * HALO, :] = s_buf[side, i, rows, :]
        at = 2 * PLANES * HALO
        out[at : at + HALO, :] = t_buf[side, rows, :]
        out[at + HALO :, :] = jnp.zeros((MSG - at - HALO, LANES), jnp.float32)


def coefficients(ja_ref, jc_ref, coef):
    for u in range(5):
        for v in range(5):
            coef[u * 5 + v] = jnp.full((TILE, LANES), ja_ref[u, v] * 2.5, jnp.float32)
            coef[25 + u * 5 + v] = jnp.full((TILE, LANES), jc_ref[u, v] * 2.5, jnp.float32)


def phases(table_ref):
    lane = lax.broadcasted_iota(jnp.int32, (TILE, LANES), 1)
    is_first, is_last = lane == 0, lane == LANES - 1
    cosine = table_ref[32:40, :]
    sine = table_ref[40:48, :]
    turn_c = jnp.where(is_first | is_last, cosine, 1.0)
    turn_s = jnp.where(is_first, -sine, jnp.where(is_last, sine, 0.0))
    return is_first, is_last, turn_c, turn_s


def tile_update(cur, base, new, forced, step, coef, omega_ref, phase, alpha, row):
    is_first, is_last, turn_c, turn_s = phase
    here = pl.ds(row, TILE)
    dt = step[here, :] * (alpha * 0.2)
    for e in range(2):
        center, axial, circ, total = [], [], [], []
        for c in range(2):
            for v in range(5):
                center.append(cur[e * 10 + c * 5 + v, here, :])
        for c in range(2):
            for v in range(5):
                i = e * 10 + c * 5 + v
                up = cur[i, pl.ds(row + 1, TILE), :]
                down = cur[i, pl.ds(row - 1, TILE), :]
                mid, other = center[c * 5 + v], center[(1 - c) * 5 + v]
                turned = turn_c * mid + turn_s * other if c == 0 else turn_c * mid - turn_s * other
                right = pltpu.roll(jnp.where(is_first, turned, mid), LANES - 1, 1)
                left = pltpu.roll(jnp.where(is_last, turned, mid), 1, 1)
                axial.append(up - down)
                circ.append(right - left)
                total.append((up + down) + (right + left))
        freq = omega_ref[e] * 5.0
        for c in range(2):
            for u in range(5):
                i = e * 10 + c * 5 + u
                acc = total[c * 5 + u] + forced[i, here, :] - 4.0 * center[c * 5 + u]
                spin = freq * center[(1 - c) * 5 + u]
                acc = acc + spin if c == 0 else acc - spin
                conv = None
                for v in range(5):
                    a = coef[u * 5 + v] * axial[c * 5 + v]
                    b = coef[25 + u * 5 + v] * circ[c * 5 + v]
                    conv = a + b if conv is None else conv + (a + b)
                new[i, here, :] = base[i, here, :] + dt * (acc - conv)


def make_moments(cell_ref, weight_ref, count_ref, moments_ref):
    faces = cell_ref.shape[1]
    modes = weight_ref.shape[0]
    cell = cell_ref[...]
    row = lax.shift_right_logical(cell, 7)
    col = jnp.bitwise_and(cell, LANES - 1)
    live = lax.broadcasted_iota(jnp.int32, (1, faces), 1) < count_ref[0]
    weight = jnp.where(live, weight_ref[...], 0.0)
    in_row = lax.broadcasted_iota(jnp.int32, (ROWS, faces), 0) == row
    in_col = (lax.broadcasted_iota(jnp.int32, (LANES, faces), 0) == col).astype(jnp.float32)
    spread = jnp.concatenate(
        [jnp.where(in_row, weight[m : m + 1, :], 0.0) for m in range(modes)], axis=0
    )
    moments_ref[...] = lax.dot_general(
        spread, in_col, (((1,), (1,)), ((), ())), precision=HIGH, preferred_element_type=jnp.float32
    )


def make_tables(ids_ref, table_ref):
    blade = lax.broadcasted_iota(jnp.int32, (1, LANES), 1)
    rows = []
    for yl, x in itertools.product(range(SIZES[1]), range(SIZES[0])):
        rows.append(blade * ids_ref[x * SIZES[1] + yl])
    product = jnp.concatenate(rows, axis=0)
    turns = ((product.astype(jnp.float32) + 0.5) * (1.0 / BLADES)).astype(jnp.int32)
    angle = 2.0 * jnp.pi * (product - turns * BLADES).astype(jnp.float32) / BLADES
    n = len(rows)
    table_ref[0:n, :] = jnp.cos(angle)
    table_ref[n : 2 * n, :] = jnp.sin(angle)
    mine = ids_ref[lax.axis_index("x") * SIZES[1] + lax.axis_index("yl")]
    sigma = jnp.full((TILE, LANES), mine, jnp.int32).astype(jnp.float32)
    sigma = 2.0 * jnp.pi * sigma / BLADES
    table_ref[2 * n : 2 * n + 8, :] = jnp.cos(sigma)
    table_ref[2 * n + 8 : 2 * n + 16, :] = jnp.sin(sigma)


def inner_kernel(
    cell_ref, weight_ref, count_ref, ids_ref, ja_ref, jc_ref, omega_ref, q_ref, s_ref, t_ref,
    moments_ref, table_ref, rim_ref, core_ref, base, first, second, forced, step, coef,
):
    make_moments(cell_ref, weight_ref, count_ref, moments_ref)
    make_tables(ids_ref, table_ref)
    coefficients(ja_ref, jc_ref, coef)
    phase = phases(table_ref)
    own = pl.ds(OWN, ROWS)
    for i in range(PLANES):
        base[i, own, :] = q_ref[i]
        forced[i, own, :] = s_ref[i] * 5.0
    step[own, :] = t_ref[...]

    bufs = (base, first, second, first, base)
    for t in range(1, LEVELS + 1):
        k = (t - 1) % SECTIONS
        cur, new = bufs[k], bufs[k + 1]
        valid = ROWS - 2 * t
        tiles = (valid + TILE - 1) // TILE

        def body(j, carry, cur=cur, new=new, alpha=ALPHAS[k], t=t, valid=valid, tiles=tiles):
            row = OWN + t + j * TILE
            tile_update(cur, base, new, forced, step, coef, omega_ref, phase, alpha, row)
            return carry

        lax.fori_loop(0, tiles, body, 0)
        if t < LEVELS:
            for i in range(PLANES):
                rim_ref[t - 1, i, 0:4, :] = new[i, OWN + t : OWN + t + 4, :]
                rim_ref[t - 1, i, 4:8, :] = new[i, OWN + ROWS - 4 - t : OWN + ROWS - t, :]
        else:
            for i in range(PLANES):
                core_ref[i] = new[i, OWN + t : OWN + ROWS - t, :]


def rim_kernel(
    ja_ref, jc_ref, omega_ref, q_ref, s_ref, t_ref, near_ref, far_ref, moments_ref, table_ref, rim_ref, core_ref,
    out_ref, force_ref, base, other, first, second, forced, step, coef,
):
    even = lax.axis_index("core") == 0
    coefficients(ja_ref, jc_ref, coef)
    phase = phases(table_ref)
    edge = jnp.zeros((4, LANES), jnp.float32)

    def put(buf, at, top, low, scale):
        near = near_ref[pl.ds(at, HALO), :]
        far = far_ref[pl.ds(at, HALO), :]
        buf[0:4, :] = edge
        buf[4:16, :] = jnp.where(even, far, near) * scale
        buf[16:PART, :] = top * scale
        buf[PART : PART + 16, :] = low * scale
        buf[PART + 16 : PART + 28, :] = jnp.where(even, near, far) * scale
        buf[PART + 28 : PART + 32, :] = edge

    for i in range(PLANES):
        put(base.at[i], i * HALO, q_ref[i, 0:16, :], q_ref[i, 16:32, :], 1.0)
        put(forced.at[i], (PLANES + i) * HALO, s_ref[i, 0:16, :], s_ref[i, 16:32, :], 5.0)
        for buf in (other, first, second):
            buf[i, 0:8, :] = jnp.zeros((8, LANES), jnp.float32)
            buf[i, PART + 24 : PART + 32, :] = jnp.zeros((8, LANES), jnp.float32)
    put(step, 2 * PLANES * HALO, t_ref[0:16, :], t_ref[16:32, :], 1.0)

    for it in range(ITERS):
        start, end = (base, other) if it % 2 == 0 else (other, base)
        bufs = (start, first, second, first, end)
        for k in range(SECTIONS):
            t = it * SECTIONS + k + 1
            cur, new = bufs[k], bufs[k + 1]
            for row in (4 + t, 8 + t, PART + 16 - t, PART + 20 - t):
                tile_update(cur, start, new, forced, step, coef, omega_ref, phase, ALPHAS[k], row)
            if t < LEVELS:
                for i in range(PLANES):
                    new[i, 16 + t : 20 + t, :] = rim_ref[t - 1, i, 0:4, :]
                    new[i, PART + 12 - t : PART + 16 - t, :] = rim_ref[t - 1, i, 4:8, :]
    for i in range(PLANES):
        out_ref[i, 0:HALO, :] = end[i, 16 : 16 + HALO, :]
        out_ref[i, HALO : ROWS - HALO, :] = core_ref[i]
        out_ref[i, ROWS - HALO : ROWS, :] = end[i, PART + 4 : PART + 16, :]

    sums = []
    modes = moments_ref.shape[0] // ROWS
    for m in range(modes):
        for ec in range(4):
            acc = None
            for r in range(0, ROWS, TILE):
                term = moments_ref[m * ROWS + r : m * ROWS + r + TILE, :] * out_ref[ec * 5 + 4, r : r + TILE, :]
                acc = term if acc is None else acc + term
            sums.append(acc)
    stacked = jnp.concatenate(sums, axis=0)
    count = len(sums)
    pick = lax.broadcasted_iota(jnp.int32, (LANES, count * TILE), 1) // TILE
    pick = (pick == lax.broadcasted_iota(jnp.int32, (LANES, count * TILE), 0)).astype(jnp.float32)
    by_lane = jnp.dot(pick, stacked, precision=HIGH, preferred_element_type=jnp.float32)
    ones = jnp.ones(force_ref.shape, jnp.float32)
    force_ref[...] = lax.dot_general(
        ones, by_lane, (((1,), (1,)), ((), ())), precision=HIGH, preferred_element_type=jnp.float32
    )


def middle_kernel(in_ref, out_ref):
    got = in_ref[...]
    mine = lax.axis_index("yl")
    lane = lax.broadcasted_iota(jnp.int32, (1, LANES), 1)
    keep = (lane % 16 < 4) & (lane < 64)
    total = None
    for yl in range(SIZES[1]):
        part = jnp.sum(got[yl * 4 : yl * 4 + 4, :], axis=0, keepdims=True)
        part = pltpu.roll(part, (LANES - 4 * mine) % LANES, 1)
        part = jnp.where(keep, part, 0.0)
        if yl:
            part = pltpu.roll(part, 4 * yl, 1)
        total = part if total is None else total + part
    out_ref[...] = jnp.broadcast_to(total, out_ref.shape)


def final_kernel(in_ref, table_ref, out_ref):
    mine = lax.axis_index("x")
    depth = SIZES[2]
    parts = [
        jnp.sum(in_ref[x * depth : (x + 1) * depth, :], axis=0, keepdims=True) for x in range(SIZES[0])
    ]
    force = pltpu.roll(jnp.concatenate(parts, axis=0), (LANES - 16 * mine) % LANES, 1)
    n = SIZES[0] * SIZES[1]
    for e in range(2):
        real, imag = None, None
        for yl in range(SIZES[1]):
            at = yl * 4 + e * 2
            f_r = force[:, at : at + 1]
            f_i = force[:, at + 1 : at + 2]
            cosine = table_ref[yl * 4 : yl * 4 + 4, :]
            sine = table_ref[n + yl * 4 : n + yl * 4 + 4, :]
            r = f_r * cosine - f_i * sine
            i = f_r * sine + f_i * cosine
            real = r if real is None else real + r
            imag = i if imag is None else imag + i
        scale = 1.0 / BLADES
        out_ref[0, 0, e : e + 1, :] = (jnp.sum(real, axis=0, keepdims=True) * scale)[:, :BLADES]
        out_ref[0, 1, e : e + 1, :] = (jnp.sum(imag, axis=0, keepdims=True) * scale)[:, :BLADES]


def shape(*dims):
    return jax.ShapeDtypeStruct(dims, jnp.float32)


VMEM = pl.BlockSpec(memory_space=pltpu.VMEM)
SMEM = pl.BlockSpec(memory_space=pltpu.SMEM)
ANY = pl.BlockSpec(memory_space=pltpu.HBM)


def call(kernel, out_shape, in_specs, scratch=(), cost=(1000, 1000)):
    return pl.pallas_call(
        kernel,
        out_shape=out_shape,
        in_specs=in_specs,
        out_specs=jax.tree.map(lambda _: VMEM, out_shape),
        scratch_shapes=list(scratch),
        compiler_params=pltpu.CompilerParams(vmem_limit_bytes=32 * 1024 * 1024),
        cost_estimate=pl.CostEstimate(flops=cost[0], bytes_accessed=cost[1], transcendentals=0),
    )


def per_device(
    perturbation, source, time_step, jac_axial, jac_circ, omega, diam_ids, surf_cell, surf_weight, face_count
):
    q = perturbation.reshape(PLANES, ROWS, LANES)
    src = source.reshape(PLANES, ROWS, LANES)
    edges = pltpu.VMEM((2, PLANES, 16, LANES), jnp.float32)
    near, far = call(
        pack_kernel,
        (shape(MSG, LANES),) * 2,
        [ANY] * 3,
        [edges, edges, pltpu.VMEM((2, 16, LANES), jnp.float32), pltpu.SemaphoreType.DMA((2, 3))],
    )(*(pltpu.with_memory_space_constraint(a, pltpu.HBM) for a in (q, src, time_step)))
    near = lax.ppermute(near, AXES, swap_pairs(True))
    far = lax.ppermute(far, AXES, swap_pairs(False))
    coef = pltpu.VMEM((50, TILE, LANES), jnp.float32)
    big = pltpu.VMEM((PLANES, ROWS + 16, LANES), jnp.float32)
    moments, table, rim, core = call(
        inner_kernel,
        (shape(16 * ROWS, LANES), shape(48, LANES), shape(LEVELS - 1, PLANES, TILE, LANES), shape(PLANES, TILE, LANES)),
        [VMEM, VMEM] + [SMEM] * 5 + [VMEM] * 3,
        [big, big, big, big, pltpu.VMEM((ROWS + 16, LANES), jnp.float32), coef],
        cost=(400_000_000, 1_000_000),
    )(surf_cell.reshape(1, -1), surf_weight, face_count, diam_ids, jac_axial, jac_circ, omega, q, src, time_step)
    big = pltpu.VMEM((PLANES, 2 * PART, LANES), jnp.float32)
    result, force = call(
        rim_kernel,
        (shape(PLANES, ROWS, LANES), shape(16, LANES)),
        [SMEM] * 3 + [VMEM] * 9,
        [big] * 5 + [pltpu.VMEM((2 * PART, LANES), jnp.float32), coef],
        cost=(100_000_000, 2_000_000),
    )(jac_axial, jac_circ, omega, q, src, time_step, near, far, moments, table, rim, core)
    got = lax.all_to_all(force, ("yl", "yh", "core"), 0, 0, tiled=True)
    middle = call(middle_kernel, shape(32, LANES), [VMEM])(got)
    got = lax.all_to_all(middle, ("x", "z"), 0, 0, tiled=True)
    influence = call(final_kernel, shape(1, 2, 2, BLADES), [VMEM, VMEM])(got, table)
    return result.reshape(perturbation.shape), influence


def solution(mesh):
    fine = Mesh(mesh.devices.reshape(SIZES), AXES)
    diam, blocks = ("x", "yl"), ("z", "yh", "core")
    in_specs = (
        P(diam, None, None, None, blocks, None),
        P(None, None, None, blocks, None),
        P(blocks, None),
        P(),
        P(),
        P(),
        P(),
        P(blocks),
        P(None, blocks),
        P(blocks),
    )
    out_specs = (P(diam, None, None, None, blocks, None), P(diam, None, None, None))
    return jax.shard_map(per_device, mesh=fine, in_specs=in_specs, out_specs=out_specs, check_vma=False)
```

```python
import itertools

import jax
import jax.numpy as jnp
from jax import lax
from jax.experimental import pallas as pl
from jax.experimental.pallas import tpu as pltpu
from jax.sharding import Mesh
from jax.sharding import PartitionSpec as P

BLADES = 72
ITERS = 3
SECTIONS = 4
HALO = ITERS * SECTIONS
ALPHAS = (0.25, 1.0 / 3.0, 0.5, 1.0)
HIGH = lax.Precision.HIGHEST
AXES = ("x", "yl", "z", "yh", "core")
SIZES = (4, 4, 8, 2, 2)
PLANES = 20
ROWS = 32
LANES = 128
MSG = 2 * PLANES * HALO + 16
LEVELS = HALO
OWN = 8
PART = 32
TILE = 8


def flat(*coords):
    out = 0
    for c, n in zip(coords, SIZES):
        out = out * n + c
    return out


def swap_pairs(same_chip):
    pairs = []
    blocks = SIZES[2] * SIZES[3] * SIZES[4]
    for x, yl, p in itertools.product(range(SIZES[0]), range(SIZES[1]), range(blocks)):
        if same_chip:
            q = p ^ 1
        else:
            q = p + 1 if p % 2 else p - 1
        if 0 <= q < blocks:
            ends = [flat(x, yl, b // 4, (b // 2) % 2, b % 2) for b in (p, q)]
            pairs.append(tuple(ends))
    return pairs


def fill_message(out, rows, q_buf, s_buf, t_buf):
    for i in range(PLANES):
        out[i * HALO : (i + 1) * HALO, :] = q_buf[i, rows, :]
        out[(PLANES + i) * HALO : (PLANES + i + 1) * HALO, :] = s_buf[i, rows, :]
    at = 2 * PLANES * HALO
    out[at : at + HALO, :] = t_buf[rows, :]
    out[at + HALO :, :] = jnp.zeros((MSG - at - HALO, LANES), jnp.float32)


def far_kernel(q_ref, s_ref, t_ref, out_ref, q_buf, s_buf, t_buf, sems):
    core = lax.axis_index("core")
    wide = q_buf.shape[1]
    rows = pl.ds(pl.multiple_of(core * (ROWS - wide), TILE), wide)
    copies = [
        pltpu.make_async_copy(q_ref.at[:, rows, :], q_buf, sems.at[0]),
        pltpu.make_async_copy(s_ref.at[:, rows, :], s_buf, sems.at[1]),
        pltpu.make_async_copy(t_ref.at[rows, :], t_buf, sems.at[2]),
    ]
    for copy in copies:
        copy.start()
    for copy in copies:
        copy.wait()
    fill_message(out_ref, pl.ds(core * (wide - HALO), HALO), q_buf, s_buf, t_buf)


def coefficients(ja_ref, jc_ref, coef):
    for u in range(5):
        for v in range(5):
            coef[u * 5 + v] = jnp.full((TILE, LANES), ja_ref[u, v] * 2.5, jnp.float32)
            coef[25 + u * 5 + v] = jnp.full((TILE, LANES), jc_ref[u, v] * 2.5, jnp.float32)


def phases(table_ref):
    lane = lax.broadcasted_iota(jnp.int32, (TILE, LANES), 1)
    is_first, is_last = lane == 0, lane == LANES - 1
    cosine = table_ref[32:40, :]
    sine = table_ref[40:48, :]
    turn_c = jnp.where(is_first | is_last, cosine, 1.0)
    turn_s = jnp.where(is_first, -sine, jnp.where(is_last, sine, 0.0))
    return is_first, is_last, turn_c, turn_s


def tile_update(cur, base, new, forced, step, coef, omega_ref, phase, alpha, row):
    is_first, is_last, turn_c, turn_s = phase
    here = pl.ds(row, TILE)
    dt = step[here, :] * (alpha * 0.2)
    for e in range(2):
        center, axial, circ, total = [], [], [], []
        for c in range(2):
            for v in range(5):
                center.append(cur[e * 10 + c * 5 + v, here, :])
        for c in range(2):
            for v in range(5):
                i = e * 10 + c * 5 + v
                up = cur[i, pl.ds(row + 1, TILE), :]
                down = cur[i, pl.ds(row - 1, TILE), :]
                mid, other = center[c * 5 + v], center[(1 - c) * 5 + v]
                turned = turn_c * mid + turn_s * other if c == 0 else turn_c * mid - turn_s * other
                right = pltpu.roll(jnp.where(is_first, turned, mid), LANES - 1, 1)
                left = pltpu.roll(jnp.where(is_last, turned, mid), 1, 1)
                axial.append(up - down)
                circ.append(right - left)
                total.append((up + down) + (right + left))
        freq = omega_ref[e] * 5.0
        for c in range(2):
            for u in range(5):
                i = e * 10 + c * 5 + u
                acc = total[c * 5 + u] + forced[i, here, :] - 4.0 * center[c * 5 + u]
                spin = freq * center[(1 - c) * 5 + u]
                acc = acc + spin if c == 0 else acc - spin
                conv = None
                for v in range(5):
                    a = coef[u * 5 + v] * axial[c * 5 + v]
                    b = coef[25 + u * 5 + v] * circ[c * 5 + v]
                    conv = a + b if conv is None else conv + (a + b)
                new[i, here, :] = base[i, here, :] + dt * (acc - conv)


def make_moments(cell_ref, weight_ref, count_ref, moments_ref):
    faces = cell_ref.shape[1]
    modes = weight_ref.shape[0]
    cell = cell_ref[...]
    row = lax.shift_right_logical(cell, 7)
    col = jnp.bitwise_and(cell, LANES - 1)
    live = lax.broadcasted_iota(jnp.int32, (1, faces), 1) < count_ref[0]
    weight = jnp.where(live, weight_ref[...], 0.0)
    in_row = lax.broadcasted_iota(jnp.int32, (ROWS, faces), 0) == row
    in_col = (lax.broadcasted_iota(jnp.int32, (LANES, faces), 0) == col).astype(jnp.float32)
    spread = jnp.concatenate(
        [jnp.where(in_row, weight[m : m + 1, :], 0.0) for m in range(modes)], axis=0
    )
    moments_ref[...] = lax.dot_general(
        spread, in_col, (((1,), (1,)), ((), ())), precision=HIGH, preferred_element_type=jnp.float32
    )


def make_tables(ids_ref, table_ref):
    blade = lax.broadcasted_iota(jnp.int32, (1, LANES), 1)
    rows = []
    for yl, x in itertools.product(range(SIZES[1]), range(SIZES[0])):
        rows.append(blade * ids_ref[x * SIZES[1] + yl])
    product = jnp.concatenate(rows, axis=0)
    turns = ((product.astype(jnp.float32) + 0.5) * (1.0 / BLADES)).astype(jnp.int32)
    angle = 2.0 * jnp.pi * (product - turns * BLADES).astype(jnp.float32) / BLADES
    n = len(rows)
    table_ref[0:n, :] = jnp.cos(angle)
    table_ref[n : 2 * n, :] = jnp.sin(angle)
    mine = ids_ref[lax.axis_index("x") * SIZES[1] + lax.axis_index("yl")]
    sigma = jnp.full((TILE, LANES), mine, jnp.int32).astype(jnp.float32)
    sigma = 2.0 * jnp.pi * sigma / BLADES
    table_ref[2 * n : 2 * n + 8, :] = jnp.cos(sigma)
    table_ref[2 * n + 8 : 2 * n + 16, :] = jnp.sin(sigma)


def inner_kernel(
    cell_ref, weight_ref, count_ref, ids_ref, ja_ref, jc_ref, omega_ref, q_ref, s_ref, t_ref,
    near_ref, moments_ref, table_ref, rim_ref, core_ref,
    base, first, second, forced, step, coef, cell, weight, sems,
):
    copies = [
        pltpu.make_async_copy(cell_ref, cell, sems.at[0]),
        pltpu.make_async_copy(weight_ref, weight, sems.at[1]),
    ]
    for copy in copies:
        copy.start()
    fill_message(near_ref, pl.ds((1 - lax.axis_index("core")) * (ROWS - HALO), HALO), q_ref, s_ref, t_ref)
    make_tables(ids_ref, table_ref)
    coefficients(ja_ref, jc_ref, coef)
    phase = phases(table_ref)
    own = pl.ds(OWN, ROWS)
    for i in range(PLANES):
        base[i, own, :] = q_ref[i]
        forced[i, own, :] = s_ref[i] * 5.0
    step[own, :] = t_ref[...]
    for copy in copies:
        copy.wait()
    make_moments(cell, weight, count_ref, moments_ref)

    bufs = (base, first, second, first, base)
    for t in range(1, LEVELS + 1):
        k = (t - 1) % SECTIONS
        cur, new = bufs[k], bufs[k + 1]
        valid = ROWS - 2 * t
        tiles = (valid + TILE - 1) // TILE

        def body(j, carry, cur=cur, new=new, alpha=ALPHAS[k], t=t, valid=valid, tiles=tiles):
            row = OWN + t + j * TILE
            tile_update(cur, base, new, forced, step, coef, omega_ref, phase, alpha, row)
            return carry

        lax.fori_loop(0, tiles, body, 0)
        if t < LEVELS:
            for i in range(PLANES):
                rim_ref[t - 1, i, 0:4, :] = new[i, OWN + t : OWN + t + 4, :]
                rim_ref[t - 1, i, 4:8, :] = new[i, OWN + ROWS - 4 - t : OWN + ROWS - t, :]
        else:
            for i in range(PLANES):
                core_ref[i] = new[i, OWN + t : OWN + ROWS - t, :]


def rim_kernel(
    ja_ref, jc_ref, omega_ref, q_ref, s_ref, t_ref, near_ref, far_ref, moments_ref, table_ref, rim_ref, core_ref,
    out_ref, force_ref, base, other, first, second, forced, step, coef,
):
    even = lax.axis_index("core") == 0
    coefficients(ja_ref, jc_ref, coef)
    phase = phases(table_ref)
    edge = jnp.zeros((4, LANES), jnp.float32)

    def put(buf, at, top, low, scale):
        near = near_ref[pl.ds(at, HALO), :]
        far = far_ref[pl.ds(at, HALO), :]
        buf[0:4, :] = edge
        buf[4:16, :] = jnp.where(even, far, near) * scale
        buf[16:PART, :] = top * scale
        buf[PART : PART + 16, :] = low * scale
        buf[PART + 16 : PART + 28, :] = jnp.where(even, near, far) * scale
        buf[PART + 28 : PART + 32, :] = edge

    for i in range(PLANES):
        put(base.at[i], i * HALO, q_ref[i, 0:16, :], q_ref[i, 16:32, :], 1.0)
        put(forced.at[i], (PLANES + i) * HALO, s_ref[i, 0:16, :], s_ref[i, 16:32, :], 5.0)
        for buf in (other, first, second):
            buf[i, 0:8, :] = jnp.zeros((8, LANES), jnp.float32)
            buf[i, PART + 24 : PART + 32, :] = jnp.zeros((8, LANES), jnp.float32)
    put(step, 2 * PLANES * HALO, t_ref[0:16, :], t_ref[16:32, :], 1.0)

    for it in range(ITERS):
        start, end = (base, other) if it % 2 == 0 else (other, base)
        bufs = (start, first, second, first, end)
        for k in range(SECTIONS):
            t = it * SECTIONS + k + 1
            cur, new = bufs[k], bufs[k + 1]
            for row in (4 + t, 8 + t, PART + 16 - t, PART + 20 - t):
                tile_update(cur, start, new, forced, step, coef, omega_ref, phase, ALPHAS[k], row)
            if t < LEVELS:
                for i in range(PLANES):
                    new[i, 16 + t : 20 + t, :] = rim_ref[t - 1, i, 0:4, :]
                    new[i, PART + 12 - t : PART + 16 - t, :] = rim_ref[t - 1, i, 4:8, :]
    for i in range(PLANES):
        out_ref[i, 0:HALO, :] = end[i, 16 : 16 + HALO, :]
        out_ref[i, HALO : ROWS - HALO, :] = core_ref[i]
        out_ref[i, ROWS - HALO : ROWS, :] = end[i, PART + 4 : PART + 16, :]

    sums = []
    modes = moments_ref.shape[0] // ROWS
    for m in range(modes):
        for ec in range(4):
            acc = None
            for r in range(0, ROWS, TILE):
                term = moments_ref[m * ROWS + r : m * ROWS + r + TILE, :] * out_ref[ec * 5 + 4, r : r + TILE, :]
                acc = term if acc is None else acc + term
            sums.append(acc)
    stacked = jnp.concatenate(sums, axis=0)
    count = len(sums)
    pick = lax.broadcasted_iota(jnp.int32, (LANES, count * TILE), 1) // TILE
    pick = (pick == lax.broadcasted_iota(jnp.int32, (LANES, count * TILE), 0)).astype(jnp.float32)
    by_lane = jnp.dot(pick, stacked, precision=HIGH, preferred_element_type=jnp.float32)
    ones = jnp.ones(force_ref.shape, jnp.float32)
    force_ref[...] = lax.dot_general(
        ones, by_lane, (((1,), (1,)), ((), ())), precision=HIGH, preferred_element_type=jnp.float32
    )


def middle_kernel(in_ref, out_ref):
    got = in_ref[...]
    mine = lax.axis_index("yl")
    lane = lax.broadcasted_iota(jnp.int32, (1, LANES), 1)
    keep = (lane % 16 < 4) & (lane < 64)
    total = None
    for yl in range(SIZES[1]):
        part = jnp.sum(got[yl * 4 : yl * 4 + 4, :], axis=0, keepdims=True)
        part = pltpu.roll(part, (LANES - 4 * mine) % LANES, 1)
        part = jnp.where(keep, part, 0.0)
        if yl:
            part = pltpu.roll(part, 4 * yl, 1)
        total = part if total is None else total + part
    out_ref[...] = jnp.broadcast_to(total, out_ref.shape)


def final_kernel(in_ref, table_ref, out_ref):
    mine = lax.axis_index("x")
    depth = SIZES[2]
    parts = [
        jnp.sum(in_ref[x * depth : (x + 1) * depth, :], axis=0, keepdims=True) for x in range(SIZES[0])
    ]
    force = pltpu.roll(jnp.concatenate(parts, axis=0), (LANES - 16 * mine) % LANES, 1)
    n = SIZES[0] * SIZES[1]
    for e in range(2):
        real, imag = None, None
        for yl in range(SIZES[1]):
            at = yl * 4 + e * 2
            f_r = force[:, at : at + 1]
            f_i = force[:, at + 1 : at + 2]
            cosine = table_ref[yl * 4 : yl * 4 + 4, :]
            sine = table_ref[n + yl * 4 : n + yl * 4 + 4, :]
            r = f_r * cosine - f_i * sine
            i = f_r * sine + f_i * cosine
            real = r if real is None else real + r
            imag = i if imag is None else imag + i
        scale = 1.0 / BLADES
        out_ref[0, 0, e : e + 1, :] = (jnp.sum(real, axis=0, keepdims=True) * scale)[:, :BLADES]
        out_ref[0, 1, e : e + 1, :] = (jnp.sum(imag, axis=0, keepdims=True) * scale)[:, :BLADES]


def shape(*dims):
    return jax.ShapeDtypeStruct(dims, jnp.float32)


VMEM = pl.BlockSpec(memory_space=pltpu.VMEM)
SMEM = pl.BlockSpec(memory_space=pltpu.SMEM)
ANY = pl.BlockSpec(memory_space=pltpu.HBM)


def call(kernel, out_shape, in_specs, scratch=(), cost=(1000, 1000)):
    return pl.pallas_call(
        kernel,
        out_shape=out_shape,
        in_specs=in_specs,
        out_specs=jax.tree.map(lambda _: VMEM, out_shape),
        scratch_shapes=list(scratch),
        compiler_params=pltpu.CompilerParams(vmem_limit_bytes=32 * 1024 * 1024),
        cost_estimate=pl.CostEstimate(flops=cost[0], bytes_accessed=cost[1], transcendentals=0),
    )


def in_hbm(value):
    return pltpu.with_memory_space_constraint(value, pltpu.HBM)


def per_device(
    perturbation, source, time_step, jac_axial, jac_circ, omega, diam_ids, surf_cell, surf_weight, face_count
):
    q = perturbation.reshape(PLANES, ROWS, LANES)
    src = source.reshape(PLANES, ROWS, LANES)
    edge = pltpu.VMEM((PLANES, 16, LANES), jnp.float32)
    far = call(
        far_kernel,
        shape(MSG, LANES),
        [ANY] * 3,
        [edge, edge, pltpu.VMEM((16, LANES), jnp.float32), pltpu.SemaphoreType.DMA((3,))],
    )(*map(in_hbm, (q, src, time_step)))
    far = lax.ppermute(far, AXES, swap_pairs(False))
    coef = pltpu.VMEM((50, TILE, LANES), jnp.float32)
    big = pltpu.VMEM((PLANES, ROWS + 16, LANES), jnp.float32)
    faces = surf_cell.shape[0]
    near, moments, table, rim, core = call(
        inner_kernel,
        (
            shape(MSG, LANES),
            shape(16 * ROWS, LANES),
            shape(48, LANES),
            shape(LEVELS - 1, PLANES, TILE, LANES),
            shape(PLANES, TILE, LANES),
        ),
        [ANY, ANY] + [SMEM] * 5 + [VMEM] * 3,
        [big, big, big, big, pltpu.VMEM((ROWS + 16, LANES), jnp.float32), coef]
        + [pltpu.VMEM((1, faces), jnp.int32), pltpu.VMEM((16, faces), jnp.float32), pltpu.SemaphoreType.DMA((2,))],
        cost=(400_000_000, 1_000_000),
    )(
        in_hbm(surf_cell.reshape(1, -1)), in_hbm(surf_weight), face_count, diam_ids,
        jac_axial, jac_circ, omega, q, src, time_step,
    )
    near = lax.ppermute(near, AXES, swap_pairs(True))
    big = pltpu.VMEM((PLANES, 2 * PART, LANES), jnp.float32)
    result, force = call(
        rim_kernel,
        (shape(PLANES, ROWS, LANES), shape(16, LANES)),
        [SMEM] * 3 + [VMEM] * 9,
        [big] * 5 + [pltpu.VMEM((2 * PART, LANES), jnp.float32), coef],
        cost=(100_000_000, 2_000_000),
    )(jac_axial, jac_circ, omega, q, src, time_step, near, far, moments, table, rim, core)
    got = lax.all_to_all(force, ("yl", "yh", "core"), 0, 0, tiled=True)
    middle = call(middle_kernel, shape(32, LANES), [VMEM])(got)
    got = lax.all_to_all(middle, ("x", "z"), 0, 0, tiled=True)
    influence = call(final_kernel, shape(1, 2, 2, BLADES), [VMEM, VMEM])(got, table)
    return result.reshape(perturbation.shape), influence


def solution(mesh):
    fine = Mesh(mesh.devices.reshape(SIZES), AXES)
    diam, blocks = ("x", "yl"), ("z", "yh", "core")
    in_specs = (
        P(diam, None, None, None, blocks, None),
        P(None, None, None, blocks, None),
        P(blocks, None),
        P(),
        P(),
        P(),
        P(),
        P(blocks),
        P(None, blocks),
        P(blocks),
    )
    out_specs = (P(diam, None, None, None, blocks, None), P(diam, None, None, None))
    return jax.shard_map(per_device, mesh=fine, in_specs=in_specs, out_specs=out_specs, check_vma=False)
```

```python
import itertools

import jax
import jax.numpy as jnp
from jax import lax
from jax.experimental import pallas as pl
from jax.experimental.pallas import tpu as pltpu
from jax.sharding import Mesh
from jax.sharding import PartitionSpec as P

BLADES = 72
ITERS = 3
SECTIONS = 4
HALO = ITERS * SECTIONS
ALPHAS = (0.25, 1.0 / 3.0, 0.5, 1.0)
HIGH = lax.Precision.HIGHEST
AXES = ("x", "yl", "z", "yh", "core")
SIZES = (4, 4, 8, 2, 2)
PLANES = 20
ROWS = 32
LANES = 128
MSG = 2 * PLANES * HALO + 16
LEVELS = HALO
OWN = 8
PART = 32
TILE = 8


def flat(*coords):
    out = 0
    for c, n in zip(coords, SIZES):
        out = out * n + c
    return out


def swap_pairs(same_chip):
    pairs = []
    blocks = SIZES[2] * SIZES[3] * SIZES[4]
    for x, yl, p in itertools.product(range(SIZES[0]), range(SIZES[1]), range(blocks)):
        if same_chip:
            q = p ^ 1
        else:
            q = p + 1 if p % 2 else p - 1
        if 0 <= q < blocks:
            ends = [flat(x, yl, b // 4, (b // 2) % 2, b % 2) for b in (p, q)]
            pairs.append(tuple(ends))
    return pairs


def fill_message(out, rows, q_buf, s_buf, t_buf):
    for i in range(PLANES):
        out[i * HALO : (i + 1) * HALO, :] = q_buf[i, rows, :]
        out[(PLANES + i) * HALO : (PLANES + i + 1) * HALO, :] = s_buf[i, rows, :]
    at = 2 * PLANES * HALO
    out[at : at + HALO, :] = t_buf[rows, :]
    out[at + HALO :, :] = jnp.zeros((MSG - at - HALO, LANES), jnp.float32)


def far_kernel(q_ref, s_ref, t_ref, out_ref, q_buf, s_buf, t_buf, sems):
    core = lax.axis_index("core")
    wide = q_buf.shape[1]
    rows = pl.ds(pl.multiple_of(core * (ROWS - wide), TILE), wide)
    copies = [
        pltpu.make_async_copy(q_ref.at[:, rows, :], q_buf, sems.at[0]),
        pltpu.make_async_copy(s_ref.at[:, rows, :], s_buf, sems.at[1]),
        pltpu.make_async_copy(t_ref.at[rows, :], t_buf, sems.at[2]),
    ]
    for copy in copies:
        copy.start()
    for copy in copies:
        copy.wait()
    fill_message(out_ref, pl.ds(core * (wide - HALO), HALO), q_buf, s_buf, t_buf)


def coefficients(ja_ref, jc_ref, coef):
    for u in range(5):
        for v in range(5):
            coef[u * 5 + v] = jnp.full((TILE, LANES), ja_ref[u, v] * 2.5, jnp.float32)
            coef[25 + u * 5 + v] = jnp.full((TILE, LANES), jc_ref[u, v] * 2.5, jnp.float32)


def phases(table_ref):
    lane = lax.broadcasted_iota(jnp.int32, (TILE, LANES), 1)
    is_first, is_last = lane == 0, lane == LANES - 1
    cosine = table_ref[32:40, :]
    sine = table_ref[40:48, :]
    turn_c = jnp.where(is_first | is_last, cosine, 1.0)
    turn_s = jnp.where(is_first, -sine, jnp.where(is_last, sine, 0.0))
    return is_first, is_last, turn_c, turn_s


def tile_update(cur, base, new, forced, step, coef, omega_ref, phase, alpha, row):
    is_first, is_last, turn_c, turn_s = phase
    here = pl.ds(row, TILE)
    dt = step[here, :] * (alpha * 0.2)
    for e in range(2):
        center, axial, circ, total = [], [], [], []
        for c in range(2):
            for v in range(5):
                center.append(cur[e * 10 + c * 5 + v, here, :])
        for c in range(2):
            for v in range(5):
                i = e * 10 + c * 5 + v
                up = cur[i, pl.ds(row + 1, TILE), :]
                down = cur[i, pl.ds(row - 1, TILE), :]
                mid, other = center[c * 5 + v], center[(1 - c) * 5 + v]
                turned = turn_c * mid + turn_s * other if c == 0 else turn_c * mid - turn_s * other
                right = pltpu.roll(jnp.where(is_first, turned, mid), LANES - 1, 1)
                left = pltpu.roll(jnp.where(is_last, turned, mid), 1, 1)
                axial.append(up - down)
                circ.append(right - left)
                total.append((up + down) + (right + left))
        freq = omega_ref[e] * 5.0
        for c in range(2):
            for u in range(5):
                i = e * 10 + c * 5 + u
                acc = total[c * 5 + u] + forced[i, here, :] - 4.0 * center[c * 5 + u]
                spin = freq * center[(1 - c) * 5 + u]
                acc = acc + spin if c == 0 else acc - spin
                conv = None
                for v in range(5):
                    a = coef[u * 5 + v] * axial[c * 5 + v]
                    b = coef[25 + u * 5 + v] * circ[c * 5 + v]
                    conv = a + b if conv is None else conv + (a + b)
                new[i, here, :] = base[i, here, :] + dt * (acc - conv)


def make_moments(cell_ref, weight_ref, count_ref, moments_ref):
    faces = cell_ref.shape[1]
    modes = weight_ref.shape[0]
    cell = cell_ref[...]
    row = lax.shift_right_logical(cell, 7)
    col = jnp.bitwise_and(cell, LANES - 1)
    live = lax.broadcasted_iota(jnp.int32, (1, faces), 1) < count_ref[0]
    weight = jnp.where(live, weight_ref[...], 0.0)
    in_row = lax.broadcasted_iota(jnp.int32, (ROWS, faces), 0) == row
    in_col = (lax.broadcasted_iota(jnp.int32, (LANES, faces), 0) == col).astype(jnp.bfloat16)
    total = None
    for _ in range(3):
        part = weight.astype(jnp.bfloat16)
        weight = weight - part.astype(jnp.float32)
        wide = part.astype(jnp.float32)
        spread = jnp.concatenate(
            [jnp.where(in_row, wide[m : m + 1, :], 0.0) for m in range(modes)], axis=0
        ).astype(jnp.bfloat16)
        term = lax.dot_general(spread, in_col, (((1,), (1,)), ((), ())), preferred_element_type=jnp.float32)
        total = term if total is None else total + term
    moments_ref[...] = total


def make_tables(ids_ref, table_ref):
    blade = lax.broadcasted_iota(jnp.int32, (1, LANES), 1)
    rows = []
    for yl, x in itertools.product(range(SIZES[1]), range(SIZES[0])):
        rows.append(blade * ids_ref[x * SIZES[1] + yl])
    product = jnp.concatenate(rows, axis=0)
    turns = ((product.astype(jnp.float32) + 0.5) * (1.0 / BLADES)).astype(jnp.int32)
    angle = 2.0 * jnp.pi * (product - turns * BLADES).astype(jnp.float32) / BLADES
    n = len(rows)
    table_ref[0:n, :] = jnp.cos(angle)
    table_ref[n : 2 * n, :] = jnp.sin(angle)
    mine = ids_ref[lax.axis_index("x") * SIZES[1] + lax.axis_index("yl")]
    sigma = jnp.full((TILE, LANES), mine, jnp.int32).astype(jnp.float32)
    sigma = 2.0 * jnp.pi * sigma / BLADES
    table_ref[2 * n : 2 * n + 8, :] = jnp.cos(sigma)
    table_ref[2 * n + 8 : 2 * n + 16, :] = jnp.sin(sigma)


def prep_kernel(cell_ref, weight_ref, ids_ref, count_ref, q_ref, s_ref, t_ref, near_ref, moments_ref, table_ref, cell, weight, ids, sems):
    copies = [
        pltpu.make_async_copy(cell_ref, cell, sems.at[0]),
        pltpu.make_async_copy(weight_ref, weight, sems.at[1]),
        pltpu.make_async_copy(ids_ref, ids, sems.at[2]),
    ]
    for copy in copies:
        copy.start()
    fill_message(near_ref, pl.ds((1 - lax.axis_index("core")) * (ROWS - HALO), HALO), q_ref, s_ref, t_ref)
    for copy in copies:
        copy.wait()
    make_tables(ids, table_ref)
    make_moments(cell, weight, count_ref, moments_ref)


def inner_kernel(
    ja_ref, jc_ref, omega_ref, q_ref, s_ref, t_ref, table_ref, rim_ref, core_ref,
    base, first, second, forced, step, coef,
):
    coefficients(ja_ref, jc_ref, coef)
    phase = phases(table_ref)
    own = pl.ds(OWN, ROWS)
    for i in range(PLANES):
        base[i, own, :] = q_ref[i]
        forced[i, own, :] = s_ref[i] * 5.0
    step[own, :] = t_ref[...]

    bufs = (base, first, second, first, base)
    for t in range(1, LEVELS + 1):
        k = (t - 1) % SECTIONS
        cur, new = bufs[k], bufs[k + 1]
        valid = ROWS - 2 * t
        tiles = (valid + TILE - 1) // TILE

        for j in range(tiles):
            tile_update(cur, base, new, forced, step, coef, omega_ref, phase, ALPHAS[k], OWN + t + j * TILE)
        if t < LEVELS:
            for i in range(PLANES):
                rim_ref[t - 1, i, 0:4, :] = new[i, OWN + t : OWN + t + 4, :]
                rim_ref[t - 1, i, 4:8, :] = new[i, OWN + ROWS - 4 - t : OWN + ROWS - t, :]
        else:
            for i in range(PLANES):
                core_ref[i] = new[i, OWN + t : OWN + ROWS - t, :]


def rim_kernel(
    ja_ref, jc_ref, omega_ref, q_ref, s_ref, t_ref, near_ref, far_ref, moments_ref, table_ref, rim_ref, core_ref,
    out_ref, force_ref, base, other, first, second, forced, step, coef, result, sem,
):
    even = lax.axis_index("core") == 0
    coefficients(ja_ref, jc_ref, coef)
    phase = phases(table_ref)
    edge = jnp.zeros((4, LANES), jnp.float32)

    def put(buf, at, top, low, scale):
        near = near_ref[pl.ds(at, HALO), :]
        far = far_ref[pl.ds(at, HALO), :]
        buf[0:4, :] = edge
        buf[4:16, :] = jnp.where(even, far, near) * scale
        buf[16:PART, :] = top * scale
        buf[PART : PART + 16, :] = low * scale
        buf[PART + 16 : PART + 28, :] = jnp.where(even, near, far) * scale
        buf[PART + 28 : PART + 32, :] = edge

    for i in range(PLANES):
        put(base.at[i], i * HALO, q_ref[i, 0:16, :], q_ref[i, 16:32, :], 1.0)
        put(forced.at[i], (PLANES + i) * HALO, s_ref[i, 0:16, :], s_ref[i, 16:32, :], 5.0)
        for buf in (other, first, second):
            buf[i, 0:8, :] = jnp.zeros((8, LANES), jnp.float32)
            buf[i, PART + 24 : PART + 32, :] = jnp.zeros((8, LANES), jnp.float32)
    put(step, 2 * PLANES * HALO, t_ref[0:16, :], t_ref[16:32, :], 1.0)

    for it in range(ITERS):
        start, end = (base, other) if it % 2 == 0 else (other, base)
        bufs = (start, first, second, first, end)
        for k in range(SECTIONS):
            t = it * SECTIONS + k + 1
            cur, new = bufs[k], bufs[k + 1]
            for row in (4 + t, 8 + t, PART + 16 - t, PART + 20 - t):
                tile_update(cur, start, new, forced, step, coef, omega_ref, phase, ALPHAS[k], row)
            if t < LEVELS:
                for i in range(PLANES):
                    new[i, 16 + t : 20 + t, :] = rim_ref[t - 1, i, 0:4, :]
                    new[i, PART + 12 - t : PART + 16 - t, :] = rim_ref[t - 1, i, 4:8, :]
    for i in range(PLANES):
        result[i, 0:HALO, :] = end[i, 16 : 16 + HALO, :]
        result[i, HALO : ROWS - HALO, :] = core_ref[i]
        result[i, ROWS - HALO : ROWS, :] = end[i, PART + 4 : PART + 16, :]
    copy = pltpu.make_async_copy(result, out_ref, sem)
    copy.start()

    sums = []
    modes = moments_ref.shape[0] // ROWS
    for m in range(modes):
        for ec in range(4):
            acc = None
            for r in range(0, ROWS, TILE):
                term = moments_ref[m * ROWS + r : m * ROWS + r + TILE, :] * result[ec * 5 + 4, r : r + TILE, :]
                acc = term if acc is None else acc + term
            sums.append(acc)
    stacked = jnp.concatenate(sums, axis=0)
    count = len(sums)
    pick = lax.broadcasted_iota(jnp.int32, (LANES, count * TILE), 1) // TILE
    pick = (pick == lax.broadcasted_iota(jnp.int32, (LANES, count * TILE), 0)).astype(jnp.float32)
    by_lane = jnp.dot(pick, stacked, precision=HIGH, preferred_element_type=jnp.float32)
    ones = jnp.ones(force_ref.shape, jnp.float32)
    force_ref[...] = lax.dot_general(
        ones, by_lane, (((1,), (1,)), ((), ())), precision=HIGH, preferred_element_type=jnp.float32
    )
    copy.wait()


def middle_kernel(in_ref, out_ref):
    got = in_ref[...]
    mine = lax.axis_index("yl")
    lane = lax.broadcasted_iota(jnp.int32, (1, LANES), 1)
    keep = (lane % 16 < 4) & (lane < 64)
    total = None
    for yl in range(SIZES[1]):
        part = jnp.sum(got[yl * 4 : yl * 4 + 4, :], axis=0, keepdims=True)
        part = pltpu.roll(part, (LANES - 4 * mine) % LANES, 1)
        part = jnp.where(keep, part, 0.0)
        if yl:
            part = pltpu.roll(part, 4 * yl, 1)
        total = part if total is None else total + part
    out_ref[...] = jnp.broadcast_to(total, out_ref.shape)


def final_kernel(in_ref, table_ref, out_ref):
    mine = lax.axis_index("x")
    depth = SIZES[2]
    parts = [
        jnp.sum(in_ref[x * depth : (x + 1) * depth, :], axis=0, keepdims=True) for x in range(SIZES[0])
    ]
    force = pltpu.roll(jnp.concatenate(parts, axis=0), (LANES - 16 * mine) % LANES, 1)
    n = SIZES[0] * SIZES[1]
    for e in range(2):
        real, imag = None, None
        for yl in range(SIZES[1]):
            at = yl * 4 + e * 2
            f_r = force[:, at : at + 1]
            f_i = force[:, at + 1 : at + 2]
            cosine = table_ref[yl * 4 : yl * 4 + 4, :]
            sine = table_ref[n + yl * 4 : n + yl * 4 + 4, :]
            r = f_r * cosine - f_i * sine
            i = f_r * sine + f_i * cosine
            real = r if real is None else real + r
            imag = i if imag is None else imag + i
        scale = 1.0 / BLADES
        out_ref[0, 0, e : e + 1, :] = (jnp.sum(real, axis=0, keepdims=True) * scale)[:, :BLADES]
        out_ref[0, 1, e : e + 1, :] = (jnp.sum(imag, axis=0, keepdims=True) * scale)[:, :BLADES]


def shape(*dims):
    return jax.ShapeDtypeStruct(dims, jnp.float32)


VMEM = pl.BlockSpec(memory_space=pltpu.VMEM)
SMEM = pl.BlockSpec(memory_space=pltpu.SMEM)
ANY = pl.BlockSpec(memory_space=pltpu.HBM)


def call(kernel, out_shape, in_specs, scratch=(), cost=(1000, 1000), out_specs=None):
    return pl.pallas_call(
        kernel,
        out_shape=out_shape,
        in_specs=in_specs,
        out_specs=out_specs or jax.tree.map(lambda _: VMEM, out_shape),
        scratch_shapes=list(scratch),
        compiler_params=pltpu.CompilerParams(vmem_limit_bytes=32 * 1024 * 1024),
        cost_estimate=pl.CostEstimate(flops=cost[0], bytes_accessed=cost[1], transcendentals=0),
    )


def in_hbm(value):
    return pltpu.with_memory_space_constraint(value, pltpu.HBM)


def per_device(
    perturbation, source, time_step, jac_axial, jac_circ, omega, diam_ids, surf_cell, surf_weight, face_count
):
    q = perturbation.reshape(PLANES, ROWS, LANES)
    src = source.reshape(PLANES, ROWS, LANES)
    edge = pltpu.VMEM((PLANES, 16, LANES), jnp.float32)
    far = call(
        far_kernel,
        shape(MSG, LANES),
        [ANY] * 3,
        [edge, edge, pltpu.VMEM((16, LANES), jnp.float32), pltpu.SemaphoreType.DMA((3,))],
    )(*map(in_hbm, (q, src, time_step)))
    far = lax.ppermute(far, AXES, swap_pairs(False))
    coef = pltpu.VMEM((50, TILE, LANES), jnp.float32)
    big = pltpu.VMEM((PLANES, ROWS + 16, LANES), jnp.float32)
    faces = surf_cell.shape[0]
    near, moments, table = call(
        prep_kernel,
        (shape(MSG, LANES), shape(16 * ROWS, LANES), shape(48, LANES)),
        [ANY] * 3 + [SMEM] + [VMEM] * 3,
        [pltpu.VMEM((1, faces), jnp.int32), pltpu.VMEM((16, faces), jnp.float32)]
        + [pltpu.SMEM(diam_ids.shape, jnp.int32), pltpu.SemaphoreType.DMA((3,))],
        cost=(400_000_000, 1_000_000),
    )(*map(in_hbm, (surf_cell.reshape(1, -1), surf_weight, diam_ids)), face_count, q, src, time_step)
    near = lax.ppermute(near, AXES, swap_pairs(True))
    rim, core = call(
        inner_kernel,
        (shape(LEVELS - 1, PLANES, TILE, LANES), shape(PLANES, TILE, LANES)),
        [SMEM] * 3 + [VMEM] * 4,
        [big, big, big, big, pltpu.VMEM((ROWS + 16, LANES), jnp.float32), coef],
        cost=(400_000_000, 1_000_000),
    )(jac_axial, jac_circ, omega, q, src, time_step, table)
    big = pltpu.VMEM((PLANES, 2 * PART, LANES), jnp.float32)
    result, force = call(
        rim_kernel,
        (shape(PLANES, ROWS, LANES), shape(16, LANES)),
        [SMEM] * 3 + [VMEM] * 9,
        [big] * 5
        + [pltpu.VMEM((2 * PART, LANES), jnp.float32), coef, pltpu.VMEM((PLANES, ROWS, LANES), jnp.float32)]
        + [pltpu.SemaphoreType.DMA],
        cost=(100_000_000, 2_000_000),
        out_specs=(ANY, VMEM),
    )(jac_axial, jac_circ, omega, q, src, time_step, near, far, moments, table, rim, core)
    got = lax.all_to_all(force, ("yl", "yh", "core"), 0, 0, tiled=True)
    middle = call(middle_kernel, shape(32, LANES), [VMEM])(got)
    got = lax.all_to_all(middle, ("x", "z"), 0, 0, tiled=True)
    influence = call(final_kernel, shape(1, 2, 2, BLADES), [VMEM, VMEM])(got, table)
    return result.reshape(perturbation.shape), influence


def solution(mesh):
    fine = Mesh(mesh.devices.reshape(SIZES), AXES)
    diam, blocks = ("x", "yl"), ("z", "yh", "core")
    in_specs = (
        P(diam, None, None, None, blocks, None),
        P(None, None, None, blocks, None),
        P(blocks, None),
        P(),
        P(),
        P(),
        P(),
        P(blocks),
        P(None, blocks),
        P(blocks),
    )
    out_specs = (P(diam, None, None, None, blocks, None), P(diam, None, None, None))
    return jax.shard_map(per_device, mesh=fine, in_specs=in_specs, out_specs=out_specs, check_vma=False)
```

```python
import itertools

import jax
import jax.numpy as jnp
from jax import lax
from jax.experimental import pallas as pl
from jax.experimental.pallas import tpu as pltpu
from jax.sharding import Mesh
from jax.sharding import PartitionSpec as P

BLADES = 72
ITERS = 3
SECTIONS = 4
HALO = ITERS * SECTIONS
ALPHAS = (0.25, 1.0 / 3.0, 0.5, 1.0)
HIGH = lax.Precision.HIGHEST
AXES = ("x", "yl", "z", "yh", "core")
SIZES = (4, 4, 8, 2, 2)
PLANES = 20
ROWS = 32
LANES = 128
SOURCE_AT = PLANES * HALO
STEP_AT = SOURCE_AT + PLANES * (HALO - 1)
MSG = STEP_AT + HALO
FAR_MSG = MSG + 8
LEVELS = HALO
OWN = 8
PART = 32
TILE = 8


def flat(*coords):
    out = 0
    for c, n in zip(coords, SIZES):
        out = out * n + c
    return out


def swap_pairs(same_chip):
    pairs = []
    blocks = SIZES[2] * SIZES[3] * SIZES[4]
    for x, yl, p in itertools.product(range(SIZES[0]), range(SIZES[1]), range(blocks)):
        if same_chip:
            q = p ^ 1
        else:
            q = p + 1 if p % 2 else p - 1
        if 0 <= q < blocks:
            ends = [flat(x, yl, b // 4, (b // 2) % 2, b % 2) for b in (p, q)]
            pairs.append(tuple(ends))
    return pairs


def fill_message(out, first, last_end, q_buf, s_buf, t_buf):
    rows = pl.ds(first, HALO)
    fewer = pl.ds(first + last_end, HALO - 1)
    for i in range(PLANES):
        out[i * HALO : (i + 1) * HALO, :] = q_buf[i, rows, :]
        at = SOURCE_AT + i * (HALO - 1)
        out[at : at + HALO - 1, :] = s_buf[i, fewer, :]
    out[STEP_AT : STEP_AT + HALO - 1, :] = t_buf[fewer, :]
    at = MSG - 1
    out[at:, :] = jnp.zeros((out.shape[0] - at, LANES), jnp.float32)


def far_kernel(q_ref, s_ref, t_ref, out_ref, q_buf, s_buf, t_buf, sems):
    core = lax.axis_index("core")
    wide = q_buf.shape[1]
    rows = pl.ds(pl.multiple_of(core * (ROWS - wide), TILE), wide)
    copies = [
        pltpu.make_async_copy(q_ref.at[:, rows, :], q_buf, sems.at[0]),
        pltpu.make_async_copy(s_ref.at[:, rows, :], s_buf, sems.at[1]),
        pltpu.make_async_copy(t_ref.at[rows, :], t_buf, sems.at[2]),
    ]
    for copy in copies:
        copy.start()
    for copy in copies:
        copy.wait()
    fill_message(out_ref, core * (wide - HALO), core, q_buf, s_buf, t_buf)


def coefficients(ja_ref, jc_ref, coef):
    for u in range(5):
        for v in range(5):
            coef[u * 5 + v] = jnp.full((TILE, LANES), ja_ref[u, v] * 2.5, jnp.float32)
            coef[25 + u * 5 + v] = jnp.full((TILE, LANES), jc_ref[u, v] * 2.5, jnp.float32)


def phases(table_ref):
    lane = lax.broadcasted_iota(jnp.int32, (TILE, LANES), 1)
    is_first, is_last = lane == 0, lane == LANES - 1
    cosine = table_ref[32:40, :]
    sine = table_ref[40:48, :]
    turn_c = jnp.where(is_first | is_last, cosine, 1.0)
    turn_s = jnp.where(is_first, -sine, jnp.where(is_last, sine, 0.0))
    return is_first, is_last, turn_c, turn_s


def tile_update(cur, base, new, forced, step, coef, omega_ref, phase, alpha, row):
    is_first, is_last, turn_c, turn_s = phase
    here = pl.ds(row, TILE)
    dt = step[here, :] * (alpha * 0.2)
    for e in range(2):
        center, axial, circ, total = [], [], [], []
        for c in range(2):
            for v in range(5):
                center.append(cur[e * 10 + c * 5 + v, here, :])
        for c in range(2):
            for v in range(5):
                i = e * 10 + c * 5 + v
                up = cur[i, pl.ds(row + 1, TILE), :]
                down = cur[i, pl.ds(row - 1, TILE), :]
                mid, other = center[c * 5 + v], center[(1 - c) * 5 + v]
                turned = turn_c * mid + turn_s * other if c == 0 else turn_c * mid - turn_s * other
                right = pltpu.roll(jnp.where(is_first, turned, mid), LANES - 1, 1)
                left = pltpu.roll(jnp.where(is_last, turned, mid), 1, 1)
                axial.append(up - down)
                circ.append(right - left)
                total.append((up + down) + (right + left))
        freq = omega_ref[e] * 5.0
        for c in range(2):
            for u in range(5):
                i = e * 10 + c * 5 + u
                acc = total[c * 5 + u] + forced[i, here, :] - 4.0 * center[c * 5 + u]
                spin = freq * center[(1 - c) * 5 + u]
                acc = acc + spin if c == 0 else acc - spin
                conv = None
                for v in range(5):
                    a = coef[u * 5 + v] * axial[c * 5 + v]
                    b = coef[25 + u * 5 + v] * circ[c * 5 + v]
                    conv = a + b if conv is None else conv + (a + b)
                new[i, here, :] = base[i, here, :] + dt * (acc - conv)


def make_moments(cell_ref, weight_ref, count_ref, moments_ref):
    faces = cell_ref.shape[1]
    modes = weight_ref.shape[0]
    cell = cell_ref[...]
    row = lax.shift_right_logical(cell, 7)
    col = jnp.bitwise_and(cell, LANES - 1)
    live = lax.broadcasted_iota(jnp.int32, (1, faces), 1) < count_ref[0]
    weight = jnp.where(live, weight_ref[...], 0.0)
    in_row = lax.broadcasted_iota(jnp.int32, (ROWS, faces), 0) == row
    in_col = (lax.broadcasted_iota(jnp.int32, (LANES, faces), 0) == col).astype(jnp.bfloat16)
    total = None
    for _ in range(3):
        part = weight.astype(jnp.bfloat16)
        weight = weight - part.astype(jnp.float32)
        wide = part.astype(jnp.float32)
        spread = jnp.concatenate(
            [jnp.where(in_row, wide[m : m + 1, :], 0.0) for m in range(modes)], axis=0
        ).astype(jnp.bfloat16)
        term = lax.dot_general(spread, in_col, (((1,), (1,)), ((), ())), preferred_element_type=jnp.float32)
        total = term if total is None else total + term
    moments_ref[...] = total


def make_tables(ids_ref, table_ref):
    blade = lax.broadcasted_iota(jnp.int32, (1, LANES), 1)
    rows = []
    for yl, x in itertools.product(range(SIZES[1]), range(SIZES[0])):
        rows.append(blade * ids_ref[x * SIZES[1] + yl])
    product = jnp.concatenate(rows, axis=0)
    turns = ((product.astype(jnp.float32) + 0.5) * (1.0 / BLADES)).astype(jnp.int32)
    angle = 2.0 * jnp.pi * (product - turns * BLADES).astype(jnp.float32) / BLADES
    n = len(rows)
    table_ref[0:n, :] = jnp.cos(angle)
    table_ref[n : 2 * n, :] = jnp.sin(angle)
    mine = ids_ref[lax.axis_index("x") * SIZES[1] + lax.axis_index("yl")]
    sigma = jnp.full((TILE, LANES), mine, jnp.int32).astype(jnp.float32)
    sigma = 2.0 * jnp.pi * sigma / BLADES
    table_ref[2 * n : 2 * n + 8, :] = jnp.cos(sigma)
    table_ref[2 * n + 8 : 2 * n + 16, :] = jnp.sin(sigma)


def prep_kernel(
    cell_ref, weight_ref, ids_ref, _, count_ref, q_ref, s_ref, t_ref, near_ref,
    moments_ref, table_ref, cell, weight, ids, sems,
):
    copies = [
        pltpu.make_async_copy(cell_ref, cell, sems.at[0]),
        pltpu.make_async_copy(weight_ref, weight, sems.at[1]),
        pltpu.make_async_copy(ids_ref, ids, sems.at[2]),
    ]
    for copy in copies:
        copy.start()
    last_end = 1 - lax.axis_index("core")
    fill_message(near_ref, last_end * (ROWS - HALO), last_end, q_ref, s_ref, t_ref)
    for copy in copies:
        copy.wait()
    make_tables(ids, table_ref)
    make_moments(cell, weight, count_ref, moments_ref)


def inner_kernel(
    ja_ref, jc_ref, omega_ref, q_ref, s_ref, t_ref, table_ref, rim_ref, core_ref,
    base, first, second, forced, step, coef,
):
    coefficients(ja_ref, jc_ref, coef)
    phase = phases(table_ref)
    own = pl.ds(OWN, ROWS)
    for i in range(PLANES):
        base[i, own, :] = q_ref[i]
        forced[i, own, :] = s_ref[i] * 5.0
    step[own, :] = t_ref[...]

    bufs = (base, first, second, first, base)
    for t in range(1, LEVELS + 1):
        k = (t - 1) % SECTIONS
        cur, new = bufs[k], bufs[k + 1]
        valid = ROWS - 2 * t
        tiles = (valid + TILE - 1) // TILE

        for j in range(tiles):
            tile_update(cur, base, new, forced, step, coef, omega_ref, phase, ALPHAS[k], OWN + t + j * TILE)
        if t < LEVELS:
            for i in range(PLANES):
                rim_ref[t - 1, i, 0:4, :] = new[i, OWN + t : OWN + t + 4, :]
                rim_ref[t - 1, i, 4:8, :] = new[i, OWN + ROWS - 4 - t : OWN + ROWS - t, :]
        else:
            for i in range(PLANES):
                core_ref[i] = new[i, OWN + t : OWN + ROWS - t, :]


def rim_sections(last_end, halo_ref, q_ref, s_ref, t_ref, rim_ref, table_ref, ja_ref, jc_ref, omega_ref, scratch):
    base, other, first, second, forced, step, coef = scratch
    coefficients(ja_ref, jc_ref, coef)
    phase = phases(table_ref)
    half = PART // 2
    taken = pl.ds(pl.multiple_of(last_end * half, half), half)
    own = pl.ds(pl.multiple_of((1 - last_end) * half, half), half)
    halo = pl.ds(jnp.where(last_end == 1, half, half - HALO), HALO)
    fewer = pl.ds(jnp.where(last_end == 1, half, half - HALO + 1), HALO - 1)
    for i in range(PLANES):
        base[i, own, :] = q_ref[i, taken, :]
        base[i, halo, :] = halo_ref[i * HALO : (i + 1) * HALO, :]
        at = SOURCE_AT + i * (HALO - 1)
        forced[i, own, :] = s_ref[i, taken, :] * 5.0
        forced[i, fewer, :] = halo_ref[at : at + HALO - 1, :] * 5.0
    step[own, :] = t_ref[taken, :]
    step[fewer, :] = halo_ref[STEP_AT : STEP_AT + HALO - 1, :]

    for it in range(ITERS):
        start, end = (base, other) if it % 2 == 0 else (other, base)
        bufs = (start, first, second, first, end)
        for k in range(SECTIONS):
            t = it * SECTIONS + k + 1
            cur, new = bufs[k], bufs[k + 1]
            row = jnp.where(last_end == 1, half - t, half - HALO + t)
            for shift in (0, HALO - TILE):
                tile_update(cur, start, new, forced, step, coef, omega_ref, phase, ALPHAS[k], row + shift)
            if t < LEVELS:
                kept = pl.ds(last_end * 4, 4)
                place = pl.ds(jnp.where(last_end == 1, half - 4 - t, half + t), 4)
                for i in range(PLANES):
                    new[i, place, :] = rim_ref[t - 1, i, kept, :]
    return end, jnp.where(last_end == 1, half - HALO, half)


def near_rim_kernel(
    ja_ref, jc_ref, omega_ref, q_ref, s_ref, t_ref, halo_ref, table_ref, rim_ref, core_ref,
    half_ref, out_ref, result, sem, *scratch,
):
    last_end = 1 - lax.axis_index("core")
    end, at = rim_sections(last_end, halo_ref, q_ref, s_ref, t_ref, rim_ref, table_ref, ja_ref, jc_ref, omega_ref, scratch)
    for i in range(PLANES):
        result[i, pl.ds(last_end * (ROWS - HALO), HALO), :] = end[i, pl.ds(at, HALO), :]
        result[i, HALO : ROWS - HALO, :] = core_ref[i]
    half = ROWS // 2
    mine = pl.ds(pl.multiple_of(last_end * half, half), half)
    copy = pltpu.make_async_copy(result.at[:, mine, :], out_ref.at[:, mine, :], sem)
    copy.start()
    for i in range(PLANES):
        half_ref[i] = result[i, mine, :]
    copy.wait()


def far_rim_kernel(
    ja_ref, jc_ref, omega_ref, q_ref, s_ref, t_ref, halo_ref, moments_ref, table_ref, rim_ref, core_ref, half_ref, _,
    out_ref, force_ref, result, sem, *scratch,
):
    last_end = lax.axis_index("core")
    end, at = rim_sections(last_end, halo_ref, q_ref, s_ref, t_ref, rim_ref, table_ref, ja_ref, jc_ref, omega_ref, scratch)
    half = ROWS // 2
    mine = pl.ds(pl.multiple_of(last_end * half, half), half)
    for i in range(PLANES):
        result[i, HALO : ROWS - HALO, :] = core_ref[i]
        result[i, pl.ds(last_end * (ROWS - HALO), HALO), :] = end[i, pl.ds(at, HALO), :]
    copy = pltpu.make_async_copy(result.at[:, mine, :], out_ref.at[:, mine, :], sem)
    copy.start()

    pressure = []
    for ec in range(4):
        i = ec * 5 + 4
        far = [result[i, pl.ds(last_end * half + r, TILE), :] for r in (0, TILE)]
        near = [half_ref[i, r : r + TILE, :] for r in (0, TILE)]
        pressure.append([jnp.where(last_end == 1, n, f) for f, n in zip(far, near)]
                        + [jnp.where(last_end == 1, f, n) for f, n in zip(far, near)])
    sums = []
    modes = moments_ref.shape[0] // ROWS
    for m in range(modes):
        for ec in range(4):
            acc = None
            for r in range(0, ROWS, TILE):
                term = moments_ref[m * ROWS + r : m * ROWS + r + TILE, :] * pressure[ec][r // TILE]
                acc = term if acc is None else acc + term
            sums.append(acc)
    stacked = jnp.concatenate(sums, axis=0)
    count = len(sums)
    pick = lax.broadcasted_iota(jnp.int32, (LANES, count * TILE), 1) // TILE
    pick = (pick == lax.broadcasted_iota(jnp.int32, (LANES, count * TILE), 0)).astype(jnp.float32)
    by_lane = jnp.dot(pick, stacked, precision=HIGH, preferred_element_type=jnp.float32)
    ones = jnp.ones(force_ref.shape, jnp.float32)
    force_ref[...] = lax.dot_general(
        ones, by_lane, (((1,), (1,)), ((), ())), precision=HIGH, preferred_element_type=jnp.float32
    )
    copy.wait()


def middle_kernel(in_ref, out_ref):
    got = in_ref[...]
    mine = lax.axis_index("yl")
    lane = lax.broadcasted_iota(jnp.int32, (1, LANES), 1)
    keep = (lane % 16 < 4) & (lane < 64)
    total = None
    for yl in range(SIZES[1]):
        part = jnp.sum(got[yl * 4 : yl * 4 + 4, :], axis=0, keepdims=True)
        part = pltpu.roll(part, (LANES - 4 * mine) % LANES, 1)
        part = jnp.where(keep, part, 0.0)
        if yl:
            part = pltpu.roll(part, 4 * yl, 1)
        total = part if total is None else total + part
    out_ref[...] = jnp.broadcast_to(total, out_ref.shape)


def final_kernel(in_ref, table_ref, out_ref):
    mine = lax.axis_index("x")
    depth = SIZES[2]
    parts = [
        jnp.sum(in_ref[x * depth : (x + 1) * depth, :], axis=0, keepdims=True) for x in range(SIZES[0])
    ]
    force = pltpu.roll(jnp.concatenate(parts, axis=0), (LANES - 16 * mine) % LANES, 1)
    n = SIZES[0] * SIZES[1]
    for e in range(2):
        real, imag = None, None
        for yl in range(SIZES[1]):
            at = yl * 4 + e * 2
            f_r = force[:, at : at + 1]
            f_i = force[:, at + 1 : at + 2]
            cosine = table_ref[yl * 4 : yl * 4 + 4, :]
            sine = table_ref[n + yl * 4 : n + yl * 4 + 4, :]
            r = f_r * cosine - f_i * sine
            i = f_r * sine + f_i * cosine
            real = r if real is None else real + r
            imag = i if imag is None else imag + i
        scale = 1.0 / BLADES
        out_ref[0, 0, e : e + 1, :] = (jnp.sum(real, axis=0, keepdims=True) * scale)[:, :BLADES]
        out_ref[0, 1, e : e + 1, :] = (jnp.sum(imag, axis=0, keepdims=True) * scale)[:, :BLADES]


def shape(*dims):
    return jax.ShapeDtypeStruct(dims, jnp.float32)


VMEM = pl.BlockSpec(memory_space=pltpu.VMEM)
SMEM = pl.BlockSpec(memory_space=pltpu.SMEM)
ANY = pl.BlockSpec(memory_space=pltpu.HBM)


def call(kernel, out_shape, in_specs, scratch=(), cost=(1000, 1000), out_specs=None, aliases=()):
    return pl.pallas_call(
        kernel,
        out_shape=out_shape,
        in_specs=in_specs,
        out_specs=out_specs or jax.tree.map(lambda _: VMEM, out_shape),
        scratch_shapes=list(scratch),
        input_output_aliases=dict(aliases),
        compiler_params=pltpu.CompilerParams(vmem_limit_bytes=32 * 1024 * 1024),
        cost_estimate=pl.CostEstimate(flops=cost[0], bytes_accessed=cost[1], transcendentals=0),
    )


def in_hbm(value):
    return pltpu.with_memory_space_constraint(value, pltpu.HBM)


def per_device(
    perturbation, source, time_step, jac_axial, jac_circ, omega, diam_ids, surf_cell, surf_weight, face_count
):
    q = perturbation.reshape(PLANES, ROWS, LANES)
    src = source.reshape(PLANES, ROWS, LANES)
    edge = pltpu.VMEM((PLANES, 16, LANES), jnp.float32)
    far = call(
        far_kernel,
        shape(FAR_MSG, LANES),
        [ANY] * 3,
        [edge, edge, pltpu.VMEM((16, LANES), jnp.float32), pltpu.SemaphoreType.DMA((3,))],
    )(*map(in_hbm, (q, src, time_step)))
    coef = pltpu.VMEM((50, TILE, LANES), jnp.float32)
    big = pltpu.VMEM((PLANES, ROWS + 16, LANES), jnp.float32)
    faces = surf_cell.shape[0]
    near, moments, table = call(
        prep_kernel,
        (shape(MSG, LANES), shape(16 * ROWS, LANES), shape(48, LANES)),
        [ANY] * 4 + [SMEM] + [VMEM] * 3,
        [pltpu.VMEM((1, faces), jnp.int32), pltpu.VMEM((16, faces), jnp.float32)]
        + [pltpu.SMEM(diam_ids.shape, jnp.int32), pltpu.SemaphoreType.DMA((3,))],
    )(*map(in_hbm, (surf_cell.reshape(1, -1), surf_weight, diam_ids)), far, face_count, q, src, time_step)
    far = lax.ppermute(far, AXES, swap_pairs(False))
    near = lax.ppermute(near, AXES, swap_pairs(True))
    rim, core = call(
        inner_kernel,
        (shape(LEVELS - 1, PLANES, TILE, LANES), shape(PLANES, TILE, LANES)),
        [SMEM] * 3 + [VMEM] * 4,
        [big, big, big, big, pltpu.VMEM((ROWS + 16, LANES), jnp.float32), coef],
    )(jac_axial, jac_circ, omega, q, src, time_step, table)
    big = pltpu.VMEM((PLANES, PART, LANES), jnp.float32)
    scratch = [pltpu.VMEM((PLANES, ROWS, LANES), jnp.float32), pltpu.SemaphoreType.DMA]
    scratch += [big] * 5 + [pltpu.VMEM((PART, LANES), jnp.float32), coef]
    half, result = call(
        near_rim_kernel,
        (shape(PLANES, ROWS // 2, LANES), shape(PLANES, ROWS, LANES)),
        [SMEM] * 3 + [VMEM] * 7,
        scratch,
        out_specs=(VMEM, ANY),
    )(jac_axial, jac_circ, omega, q, src, time_step, near, table, rim, core)
    result, force = call(
        far_rim_kernel,
        (shape(PLANES, ROWS, LANES), shape(16, LANES)),
        [SMEM] * 3 + [VMEM] * 9 + [ANY],
        scratch,
        out_specs=(ANY, VMEM),
        aliases={12: 0},
    )(jac_axial, jac_circ, omega, q, src, time_step, far, moments, table, rim, core, half, result)
    got = lax.all_to_all(force, ("yl", "yh", "core"), 0, 0, tiled=True)
    middle = call(middle_kernel, shape(32, LANES), [VMEM])(got)
    got = lax.all_to_all(middle, ("x", "z"), 0, 0, tiled=True)
    influence = call(final_kernel, shape(1, 2, 2, BLADES), [VMEM, VMEM])(got, table)
    return result.reshape(perturbation.shape), influence


def solution(mesh):
    fine = Mesh(mesh.devices.reshape(SIZES), AXES)
    diam, blocks = ("x", "yl"), ("z", "yh", "core")
    in_specs = (
        P(diam, None, None, None, blocks, None),
        P(None, None, None, blocks, None),
        P(blocks, None),
        P(),
        P(),
        P(),
        P(),
        P(blocks),
        P(None, blocks),
        P(blocks),
    )
    out_specs = (P(diam, None, None, None, blocks, None), P(diam, None, None, None))
    return jax.shard_map(per_device, mesh=fine, in_specs=in_specs, out_specs=out_specs, check_vma=False)
```

```python
import itertools

import jax
import jax.numpy as jnp
from jax import lax
from jax.experimental import pallas as pl
from jax.experimental.pallas import tpu as pltpu
from jax.sharding import Mesh
from jax.sharding import PartitionSpec as P

BLADES = 72
ITERS = 3
SECTIONS = 4
HALO = ITERS * SECTIONS
ALPHAS = (0.25, 1.0 / 3.0, 0.5, 1.0)
HIGH = lax.Precision.HIGHEST
AXES = ("x", "yl", "z", "yh", "core")
SIZES = (4, 4, 8, 2, 2)
PLANES = 20
ROWS = 32
LANES = 128
SOURCE_AT = PLANES * HALO
STEP_AT = SOURCE_AT + PLANES * (HALO - 1)
MSG = STEP_AT + HALO
FAR_MSG = MSG + 8
LEVELS = HALO
OWN = 8
PART = 32
TILE = 8


def flat(*coords):
    out = 0
    for c, n in zip(coords, SIZES):
        out = out * n + c
    return out


def swap_pairs(same_chip):
    pairs = []
    blocks = SIZES[2] * SIZES[3] * SIZES[4]
    for x, yl, p in itertools.product(range(SIZES[0]), range(SIZES[1]), range(blocks)):
        if same_chip:
            q = p ^ 1
        else:
            q = p + 1 if p % 2 else p - 1
        if 0 <= q < blocks:
            ends = [flat(x, yl, b // 4, (b // 2) % 2, b % 2) for b in (p, q)]
            pairs.append(tuple(ends))
    return pairs


def fill_message(out, first, last_end, q_buf, s_buf, t_buf):
    rows = pl.ds(first, HALO)
    fewer = pl.ds(first + last_end, HALO - 1)
    for i in range(PLANES):
        out[i * HALO : (i + 1) * HALO, :] = q_buf[i, rows, :]
        at = SOURCE_AT + i * (HALO - 1)
        out[at : at + HALO - 1, :] = s_buf[i, fewer, :]
    out[STEP_AT : STEP_AT + HALO - 1, :] = t_buf[fewer, :]
    at = MSG - 1
    out[at:, :] = jnp.zeros((out.shape[0] - at, LANES), jnp.float32)


def far_kernel(q_ref, s_ref, t_ref, out_ref, q_buf, s_buf, t_buf, sems):
    core = lax.axis_index("core")
    wide = q_buf.shape[1]
    rows = pl.ds(pl.multiple_of(core * (ROWS - wide), TILE), wide)
    copies = [
        pltpu.make_async_copy(q_ref.at[:, rows, :], q_buf, sems.at[0]),
        pltpu.make_async_copy(s_ref.at[:, rows, :], s_buf, sems.at[1]),
        pltpu.make_async_copy(t_ref.at[rows, :], t_buf, sems.at[2]),
    ]
    for copy in copies:
        copy.start()
    for copy in copies:
        copy.wait()
    fill_message(out_ref, core * (wide - HALO), core, q_buf, s_buf, t_buf)


def make_coefficients(ja, jc, omega, coef_ref):
    def put(at, value):
        coef_ref[at] = jnp.broadcast_to(value, (TILE, LANES))

    for u in range(5):
        for v in range(5):
            put(u * 5 + v, ja[u : u + 1, v : v + 1] * 2.5)
            put(25 + u * 5 + v, jc[u : u + 1, v : v + 1] * 2.5)
    for e in range(2):
        put(50 + e, omega[:, e : e + 1] * 5.0)


def phases(table_ref):
    lane = lax.broadcasted_iota(jnp.int32, (TILE, LANES), 1)
    is_first, is_last = lane == 0, lane == LANES - 1
    cosine = table_ref[32:40, :]
    sine = table_ref[40:48, :]
    turn_c = jnp.where(is_first | is_last, cosine, 1.0)
    turn_s = jnp.where(is_first, -sine, jnp.where(is_last, sine, 0.0))
    return is_first, is_last, turn_c, turn_s


def tile_update(cur, base, new, forced, step, coef, phase, alpha, row):
    is_first, is_last, turn_c, turn_s = phase
    here = pl.ds(row, TILE)
    dt = step[here, :] * (alpha * 0.2)
    for e in range(2):
        center, axial, circ, total = [], [], [], []
        for c in range(2):
            for v in range(5):
                center.append(cur[e * 10 + c * 5 + v, here, :])
        for c in range(2):
            for v in range(5):
                i = e * 10 + c * 5 + v
                up = cur[i, pl.ds(row + 1, TILE), :]
                down = cur[i, pl.ds(row - 1, TILE), :]
                mid, other = center[c * 5 + v], center[(1 - c) * 5 + v]
                turned = turn_c * mid + turn_s * other if c == 0 else turn_c * mid - turn_s * other
                right = pltpu.roll(jnp.where(is_first, turned, mid), LANES - 1, 1)
                left = pltpu.roll(jnp.where(is_last, turned, mid), 1, 1)
                axial.append(up - down)
                circ.append(right - left)
                total.append((up + down) + (right + left))
        freq = coef[50 + e]
        for c in range(2):
            for u in range(5):
                i = e * 10 + c * 5 + u
                acc = total[c * 5 + u] + forced[i, here, :] - 4.0 * center[c * 5 + u]
                spin = freq * center[(1 - c) * 5 + u]
                acc = acc + spin if c == 0 else acc - spin
                conv = None
                for v in range(5):
                    a = coef[u * 5 + v] * axial[c * 5 + v]
                    b = coef[25 + u * 5 + v] * circ[c * 5 + v]
                    conv = a + b if conv is None else conv + (a + b)
                new[i, here, :] = base[i, here, :] + dt * (acc - conv)


def make_moments(cell_ref, weight_ref, count_ref, moments_ref):
    faces = cell_ref.shape[1]
    modes = weight_ref.shape[0]
    cell = cell_ref[...]
    row = lax.shift_right_logical(cell, 7)
    col = jnp.bitwise_and(cell, LANES - 1)
    live = lax.broadcasted_iota(jnp.int32, (1, faces), 1) < count_ref[0]
    weight = jnp.where(live, weight_ref[...], 0.0)
    in_row = lax.broadcasted_iota(jnp.int32, (ROWS, faces), 0) == row
    in_col = (lax.broadcasted_iota(jnp.int32, (LANES, faces), 0) == col).astype(jnp.bfloat16)
    total = None
    for _ in range(3):
        part = weight.astype(jnp.bfloat16)
        weight = weight - part.astype(jnp.float32)
        wide = part.astype(jnp.float32)
        spread = jnp.concatenate(
            [jnp.where(in_row, wide[m : m + 1, :], 0.0) for m in range(modes)], axis=0
        ).astype(jnp.bfloat16)
        term = lax.dot_general(spread, in_col, (((1,), (1,)), ((), ())), preferred_element_type=jnp.float32)
        total = term if total is None else total + term
    moments_ref[...] = total


def make_tables(ids_ref, table_ref):
    blade = lax.broadcasted_iota(jnp.int32, (1, LANES), 1)
    rows = []
    for yl, x in itertools.product(range(SIZES[1]), range(SIZES[0])):
        rows.append(blade * ids_ref[x * SIZES[1] + yl])
    product = jnp.concatenate(rows, axis=0)
    turns = ((product.astype(jnp.float32) + 0.5) * (1.0 / BLADES)).astype(jnp.int32)
    angle = 2.0 * jnp.pi * (product - turns * BLADES).astype(jnp.float32) / BLADES
    n = len(rows)
    table_ref[0:n, :] = jnp.cos(angle)
    table_ref[n : 2 * n, :] = jnp.sin(angle)
    mine = ids_ref[lax.axis_index("x") * SIZES[1] + lax.axis_index("yl")]
    sigma = jnp.full((TILE, LANES), mine, jnp.int32).astype(jnp.float32)
    sigma = 2.0 * jnp.pi * sigma / BLADES
    table_ref[2 * n : 2 * n + 8, :] = jnp.cos(sigma)
    table_ref[2 * n + 8 : 2 * n + 16, :] = jnp.sin(sigma)


def prep_kernel(
    cell_ref, weight_ref, ids_ref, ja_ref, jc_ref, omega_ref, _, count_ref, q_ref, s_ref, t_ref, near_ref,
    moments_ref, table_ref, coef_ref, cell, weight, ids, ja, jc, omega, sems,
):
    pairs = ((cell_ref, cell), (weight_ref, weight), (ids_ref, ids), (ja_ref, ja), (jc_ref, jc), (omega_ref, omega))
    copies = [pltpu.make_async_copy(a, b, sems.at[i]) for i, (a, b) in enumerate(pairs)]
    for copy in copies:
        copy.start()
    last_end = 1 - lax.axis_index("core")
    fill_message(near_ref, last_end * (ROWS - HALO), last_end, q_ref, s_ref, t_ref)
    for copy in copies:
        copy.wait()
    make_coefficients(ja, jc, omega, coef_ref)
    make_tables(ids, table_ref)
    make_moments(cell, weight, count_ref, moments_ref)


def inner_kernel(
    coef, q_ref, s_ref, t_ref, table_ref, rim_ref, core_ref, base, first, second, forced, step,
):
    phase = phases(table_ref)
    own = pl.ds(OWN, ROWS)
    for i in range(PLANES):
        base[i, own, :] = q_ref[i]
        forced[i, own, :] = s_ref[i] * 5.0
    step[own, :] = t_ref[...]

    bufs = (base, first, second, first, base)
    for t in range(1, LEVELS + 1):
        k = (t - 1) % SECTIONS
        cur, new = bufs[k], bufs[k + 1]
        valid = ROWS - 2 * t
        tiles = (valid + TILE - 1) // TILE

        for j in range(tiles):
            tile_update(cur, base, new, forced, step, coef, phase, ALPHAS[k], OWN + t + j * TILE)
        if t < LEVELS:
            for i in range(PLANES):
                rim_ref[t - 1, i, 0:4, :] = new[i, OWN + t : OWN + t + 4, :]
                rim_ref[t - 1, i, 4:8, :] = new[i, OWN + ROWS - 4 - t : OWN + ROWS - t, :]
        else:
            for i in range(PLANES):
                core_ref[i] = new[i, OWN + t : OWN + ROWS - t, :]


def rim_sections(last_end, halo_ref, q_ref, s_ref, t_ref, rim_ref, table_ref, coef, scratch):
    base, other, first, second, forced, step = scratch
    phase = phases(table_ref)
    half = PART // 2
    taken = pl.ds(pl.multiple_of(last_end * half, half), half)
    own = pl.ds(pl.multiple_of((1 - last_end) * half, half), half)
    halo = pl.ds(jnp.where(last_end == 1, half, half - HALO), HALO)
    fewer = pl.ds(jnp.where(last_end == 1, half, half - HALO + 1), HALO - 1)
    for i in range(PLANES):
        base[i, own, :] = q_ref[i, taken, :]
        base[i, halo, :] = halo_ref[i * HALO : (i + 1) * HALO, :]
        at = SOURCE_AT + i * (HALO - 1)
        forced[i, own, :] = s_ref[i, taken, :] * 5.0
        forced[i, fewer, :] = halo_ref[at : at + HALO - 1, :] * 5.0
    step[own, :] = t_ref[taken, :]
    step[fewer, :] = halo_ref[STEP_AT : STEP_AT + HALO - 1, :]

    for it in range(ITERS):
        start, end = (base, other) if it % 2 == 0 else (other, base)
        bufs = (start, first, second, first, end)
        for k in range(SECTIONS):
            t = it * SECTIONS + k + 1
            cur, new = bufs[k], bufs[k + 1]
            row = jnp.where(last_end == 1, half - t, half - HALO + t)
            for shift in (0, HALO - TILE):
                tile_update(cur, start, new, forced, step, coef, phase, ALPHAS[k], row + shift)
            if t < LEVELS:
                kept = pl.ds(last_end * 4, 4)
                place = pl.ds(jnp.where(last_end == 1, half - 4 - t, half + t), 4)
                for i in range(PLANES):
                    new[i, place, :] = rim_ref[t - 1, i, kept, :]
    return end, jnp.where(last_end == 1, half - HALO, half)


def reduce_to_lanes(items):
    sublane = lax.broadcasted_iota(jnp.int32, (TILE, LANES), 0)
    lane = lax.broadcasted_iota(jnp.int32, (TILE, LANES), 1)
    for axis, index, shifts in ((0, sublane, (4, 2, 1)), (1, lane, (64, 32, 16))):
        size = (TILE, LANES)[axis]
        for shift in shifts:
            low = jnp.bitwise_and(index, shift) == 0
            n = len(items) // 2
            items = [
                jnp.where(low, a + pltpu.roll(a, size - shift, axis), b + pltpu.roll(b, shift, axis))
                for a, b in zip(items[:n], items[n:])
            ]
    total = items[0]
    for shift in (8, 4, 2, 1):
        low = jnp.bitwise_and(lane, shift) == 0
        total = total + jnp.where(low, pltpu.roll(total, LANES - shift, 1), pltpu.roll(total, shift, 1))
    kept = jnp.where(jnp.bitwise_and(lane, 15) == sublane, total, 0.0)
    return jnp.sum(kept, axis=0, keepdims=True)


def near_rim_kernel(coef, q_ref, s_ref, t_ref, halo_ref, table_ref, rim_ref, core_ref, half_ref, *scratch):
    last_end = 1 - lax.axis_index("core")
    end, at = rim_sections(last_end, halo_ref, q_ref, s_ref, t_ref, rim_ref, table_ref, coef, scratch)
    fill_half(last_end, end, at, core_ref, half_ref)


def fill_half(last_end, end, at, core_ref, half_ref):
    for i in range(PLANES):
        half_ref[i, pl.ds(last_end * 4, HALO), :] = end[i, pl.ds(at, HALO), :]
        half_ref[i, pl.ds((1 - last_end) * HALO, 4), :] = core_ref[i, pl.ds(last_end * 4, 4), :]


def half_of(ref, last_end):
    half = ROWS // 2
    return ref.at[:, pl.ds(pl.multiple_of(last_end * half, half), half), :]


def far_rim_kernel(
    coef, q_ref, s_ref, t_ref, halo_ref, moments_ref, table_ref, rim_ref, core_ref, near_ref,
    out_ref, half_ref, force_ref, sem, *scratch,
):
    last_end = lax.axis_index("core")
    copy = pltpu.make_async_copy(near_ref, half_of(out_ref, 1 - last_end), sem)
    copy.start()
    end, at = rim_sections(last_end, halo_ref, q_ref, s_ref, t_ref, rim_ref, table_ref, coef, scratch)
    fill_half(last_end, end, at, core_ref, half_ref)

    pressure = []
    for ec in range(4):
        i = ec * 5 + 4
        far = [half_ref[i, r : r + TILE, :] for r in (0, TILE)]
        near = [near_ref[i, r : r + TILE, :] for r in (0, TILE)]
        pressure.append([jnp.where(last_end == 1, n, f) for f, n in zip(far, near)]
                        + [jnp.where(last_end == 1, f, n) for f, n in zip(far, near)])
    items = []
    for at in range(64):
        g, ec, odd = at % 8, at // 8 % 4, at // 32
        m = g // 2 * 4 + g % 2 * 2 + odd
        acc = None
        for r in range(0, ROWS, TILE):
            term = moments_ref[m * ROWS + r : m * ROWS + r + TILE, :] * pressure[ec][r // TILE]
            acc = term if acc is None else acc + term
        items.append(acc)
    force_ref[...] = jnp.broadcast_to(reduce_to_lanes(items), force_ref.shape)
    copy.wait()


def middle_kernel(in_ref, out_ref):
    got = in_ref[...]
    mine = lax.axis_index("yl")
    lane = lax.broadcasted_iota(jnp.int32, (1, LANES), 1)
    keep = lane % 32 < 4
    at = mine // 2 * 16 + mine % 2 * 4
    total = None
    for yl in range(SIZES[1]):
        part = jnp.sum(got[yl * 4 : yl * 4 + 4, :], axis=0, keepdims=True)
        part = pltpu.roll(part, (LANES - at) % LANES, 1)
        part = jnp.where(keep, part, 0.0)
        if yl:
            part = pltpu.roll(part, 4 * yl, 1)
        total = part if total is None else total + part
    out_ref[...] = jnp.broadcast_to(total, out_ref.shape)


def final_kernel(in_ref, table_ref, half_ref, _, out_ref, result_ref, sem):
    copy = pltpu.make_async_copy(half_ref, half_of(result_ref, lax.axis_index("core")), sem)
    copy.start()
    mine = lax.axis_index("x")
    depth = SIZES[2]
    parts = [
        jnp.sum(in_ref[x * depth : (x + 1) * depth, :], axis=0, keepdims=True) for x in range(SIZES[0])
    ]
    force = pltpu.roll(jnp.concatenate(parts, axis=0), (LANES - 32 * mine) % LANES, 1)
    n = SIZES[0] * SIZES[1]
    for e in range(2):
        real, imag = None, None
        for yl in range(SIZES[1]):
            at = yl * 4 + e * 2
            f_r = force[:, at : at + 1]
            f_i = force[:, at + 1 : at + 2]
            cosine = table_ref[yl * 4 : yl * 4 + 4, :]
            sine = table_ref[n + yl * 4 : n + yl * 4 + 4, :]
            r = f_r * cosine - f_i * sine
            i = f_r * sine + f_i * cosine
            real = r if real is None else real + r
            imag = i if imag is None else imag + i
        scale = 1.0 / BLADES
        out_ref[0, 0, e : e + 1, :] = (jnp.sum(real, axis=0, keepdims=True) * scale)[:, :BLADES]
        out_ref[0, 1, e : e + 1, :] = (jnp.sum(imag, axis=0, keepdims=True) * scale)[:, :BLADES]
    copy.wait()


def shape(*dims):
    return jax.ShapeDtypeStruct(dims, jnp.float32)


VMEM = pl.BlockSpec(memory_space=pltpu.VMEM)
SMEM = pl.BlockSpec(memory_space=pltpu.SMEM)
ANY = pl.BlockSpec(memory_space=pltpu.HBM)


def call(kernel, out_shape, in_specs, scratch=(), cost=(1000, 1000), out_specs=None, aliases=()):
    return pl.pallas_call(
        kernel,
        out_shape=out_shape,
        in_specs=in_specs,
        out_specs=out_specs or jax.tree.map(lambda _: VMEM, out_shape),
        scratch_shapes=list(scratch),
        input_output_aliases=dict(aliases),
        compiler_params=pltpu.CompilerParams(vmem_limit_bytes=32 * 1024 * 1024),
        cost_estimate=pl.CostEstimate(flops=cost[0], bytes_accessed=cost[1], transcendentals=0),
    )


def in_hbm(value):
    return pltpu.with_memory_space_constraint(value, pltpu.HBM)


def per_device(
    perturbation, source, time_step, jac_axial, jac_circ, omega, diam_ids, surf_cell, surf_weight, face_count
):
    q = perturbation.reshape(PLANES, ROWS, LANES)
    src = source.reshape(PLANES, ROWS, LANES)
    edge = pltpu.VMEM((PLANES, 16, LANES), jnp.float32)
    far = call(
        far_kernel,
        shape(FAR_MSG, LANES),
        [ANY] * 3,
        [edge, edge, pltpu.VMEM((16, LANES), jnp.float32), pltpu.SemaphoreType.DMA((3,))],
    )(*map(in_hbm, (q, src, time_step)))
    big = pltpu.VMEM((PLANES, ROWS + 16, LANES), jnp.float32)
    faces = surf_cell.shape[0]
    near, moments, table, coef = call(
        prep_kernel,
        (shape(MSG, LANES), shape(16 * ROWS, LANES), shape(48, LANES), shape(52, TILE, LANES)),
        [ANY] * 7 + [SMEM] + [VMEM] * 3,
        [pltpu.VMEM((1, faces), jnp.int32), pltpu.VMEM((16, faces), jnp.float32)]
        + [pltpu.SMEM(diam_ids.shape, jnp.int32), pltpu.VMEM((5, 5), jnp.float32), pltpu.VMEM((5, 5), jnp.float32)]
        + [pltpu.VMEM((1, 2), jnp.float32), pltpu.SemaphoreType.DMA((6,))],
    )(
        *map(in_hbm, (surf_cell.reshape(1, -1), surf_weight, diam_ids, jac_axial, jac_circ, omega.reshape(1, 2))),
        far, face_count, q, src, time_step,
    )
    far = lax.ppermute(far, AXES, swap_pairs(False))
    near = lax.ppermute(near, AXES, swap_pairs(True))
    rim, core = call(
        inner_kernel,
        (shape(LEVELS - 1, PLANES, TILE, LANES), shape(PLANES, TILE, LANES)),
        [VMEM] * 5,
        [big, big, big, big, pltpu.VMEM((ROWS + 16, LANES), jnp.float32)],
    )(coef, q, src, time_step, table)
    big = pltpu.VMEM((PLANES, PART, LANES), jnp.float32)
    scratch = [big] * 5 + [pltpu.VMEM((PART, LANES), jnp.float32)]
    half = shape(PLANES, ROWS // 2, LANES)
    near_half = call(near_rim_kernel, half, [VMEM] * 8, scratch)(coef, q, src, time_step, near, table, rim, core)
    result, far_half, force = call(
        far_rim_kernel,
        (shape(PLANES, ROWS, LANES), half, shape(16, LANES)),
        [VMEM] * 10,
        [pltpu.SemaphoreType.DMA] + scratch,
        out_specs=(ANY, VMEM, VMEM),
    )(coef, q, src, time_step, far, moments, table, rim, core, near_half)
    got = lax.all_to_all(force, ("yl", "yh", "core"), 0, 0, tiled=True)
    middle = call(middle_kernel, shape(32, LANES), [VMEM])(got)
    got = lax.all_to_all(middle, ("x", "z"), 0, 0, tiled=True)
    influence, result = call(
        final_kernel,
        (shape(1, 2, 2, BLADES), shape(PLANES, ROWS, LANES)),
        [VMEM] * 3 + [ANY],
        [pltpu.SemaphoreType.DMA],
        out_specs=(VMEM, ANY),
        aliases={3: 1},
    )(got, table, far_half, result)
    return result.reshape(perturbation.shape), influence


def solution(mesh):
    fine = Mesh(mesh.devices.reshape(SIZES), AXES)
    diam, blocks = ("x", "yl"), ("z", "yh", "core")
    in_specs = (
        P(diam, None, None, None, blocks, None),
        P(None, None, None, blocks, None),
        P(blocks, None),
        P(),
        P(),
        P(),
        P(),
        P(blocks),
        P(None, blocks),
        P(blocks),
    )
    out_specs = (P(diam, None, None, None, blocks, None), P(diam, None, None, None))
    return jax.shard_map(per_device, mesh=fine, in_specs=in_specs, out_specs=out_specs, check_vma=False)
```

```python
import itertools

import jax
import jax.numpy as jnp
from jax import lax
from jax.experimental import pallas as pl
from jax.experimental.pallas import tpu as pltpu
from jax.sharding import Mesh
from jax.sharding import PartitionSpec as P

BLADES = 72
ITERS = 3
SECTIONS = 4
HALO = ITERS * SECTIONS
ALPHAS = (0.25, 1.0 / 3.0, 0.5, 1.0)
HIGH = lax.Precision.HIGHEST
AXES = ("x", "yl", "z", "yh", "core")
SIZES = (4, 4, 8, 2, 2)
PLANES = 20
ROWS = 32
LANES = 128
SOURCE_AT = PLANES * HALO
STEP_AT = SOURCE_AT + PLANES * (HALO - 1)
MSG = STEP_AT + HALO
FAR_MSG = MSG + 8
LEVELS = HALO
OWN = 8
RIM = 48
TILE = 8


def flat(*coords):
    out = 0
    for c, n in zip(coords, SIZES):
        out = out * n + c
    return out


def swap_pairs(same_chip):
    pairs = []
    blocks = SIZES[2] * SIZES[3] * SIZES[4]
    for x, yl, p in itertools.product(range(SIZES[0]), range(SIZES[1]), range(blocks)):
        if same_chip:
            q = p ^ 1
        else:
            q = p + 1 if p % 2 else p - 1
        if 0 <= q < blocks:
            ends = [flat(x, yl, b // 4, (b // 2) % 2, b % 2) for b in (p, q)]
            pairs.append(tuple(ends))
    return pairs


def fill_message(out, first, last_end, q_buf, s_buf, t_buf):
    rows = pl.ds(first, HALO)
    fewer = pl.ds(first + last_end, HALO - 1)
    for i in range(PLANES):
        out[i * HALO : (i + 1) * HALO, :] = q_buf[i, rows, :]
        at = SOURCE_AT + i * (HALO - 1)
        out[at : at + HALO - 1, :] = s_buf[i, fewer, :]
    out[STEP_AT : STEP_AT + HALO - 1, :] = t_buf[fewer, :]
    at = MSG - 1
    out[at:, :] = jnp.zeros((out.shape[0] - at, LANES), jnp.float32)


def far_kernel(q_ref, s_ref, t_ref, out_ref, q_buf, s_buf, t_buf, sems):
    core = lax.axis_index("core")
    wide = q_buf.shape[1]
    rows = pl.ds(pl.multiple_of(core * (ROWS - wide), TILE), wide)
    piece = PLANES // 4
    copies = [pltpu.make_async_copy(t_ref.at[rows, :], t_buf, sems.at[8])]
    for i in range(4):
        some = slice(i * piece, (i + 1) * piece)
        copies.append(pltpu.make_async_copy(q_ref.at[some, rows, :], q_buf.at[some], sems.at[i]))
        copies.append(pltpu.make_async_copy(s_ref.at[some, rows, :], s_buf.at[some], sems.at[4 + i]))
    for copy in copies:
        copy.start()
    for copy in copies:
        copy.wait()
    fill_message(out_ref, core * (wide - HALO), core, q_buf, s_buf, t_buf)


def make_coefficients(ja, jc, omega, coef_ref):
    def put(at, value):
        coef_ref[at] = jnp.broadcast_to(value, (TILE, LANES))

    for u in range(5):
        for v in range(5):
            put(u * 5 + v, ja[u : u + 1, v : v + 1] * 2.5)
            put(25 + u * 5 + v, jc[u : u + 1, v : v + 1] * 2.5)
    for e in range(2):
        put(50 + e, omega[:, e : e + 1] * 5.0)


def phases(table_ref):
    lane = lax.broadcasted_iota(jnp.int32, (TILE, LANES), 1)
    is_first, is_last = lane == 0, lane == LANES - 1
    cosine = table_ref[32:40, :]
    sine = table_ref[40:48, :]
    turn_c = jnp.where(is_first | is_last, cosine, 1.0)
    turn_s = jnp.where(is_first, -sine, jnp.where(is_last, sine, 0.0))
    return is_first, is_last, turn_c, turn_s


def block_update(load, store, freq, dt, coef, phase):
    is_first, is_last, turn_c, turn_s = phase
    center = [load("cur", p, 0) for p in range(10)]
    axial, circ, total = [], [], []
    for p in range(10):
        up, down = load("cur", p, 1), load("cur", p, -1)
        mid, other = center[p], center[(p + 5) % 10]
        turned = turn_c * mid + turn_s * other if p < 5 else turn_c * mid - turn_s * other
        right = pltpu.roll(jnp.where(is_first, turned, mid), LANES - 1, 1)
        left = pltpu.roll(jnp.where(is_last, turned, mid), 1, 1)
        axial.append(up - down)
        circ.append(right - left)
        total.append((up + down) + (right + left))
    for p in range(10):
        c, u = divmod(p, 5)
        acc = total[p] + load("forced", p, 0) - 4.0 * center[p]
        spin = freq * center[(p + 5) % 10]
        acc = acc + spin if c == 0 else acc - spin
        conv = None
        for v in range(5):
            a = coef[u * 5 + v] * axial[c * 5 + v]
            b = coef[25 + u * 5 + v] * circ[c * 5 + v]
            conv = a + b if conv is None else conv + (a + b)
        store(p, load("base", p, 0) + dt * (acc - conv))


def tile_update(cur, base, new, forced, step, coef, phase, alpha, row):
    refs = dict(cur=cur, base=base, forced=forced)
    here = pl.ds(row, TILE)
    dt = step[here, :] * (alpha * 0.2)
    for e in range(2):

        def load(kind, p, shift, e=e):
            return refs[kind][e * 10 + p, pl.ds(row + shift, TILE), :]

        def store(p, value, e=e):
            new[e * 10 + p, here, :] = value

        block_update(load, store, coef[50 + e], dt, coef, phase)


def mixed_update(cur, base, new, forced, step, coef, phase, alpha, row):
    refs = dict(cur=cur, base=base, forced=forced)
    upper = lax.broadcasted_iota(jnp.int32, (TILE, LANES), 0) < 4
    places = (pl.ds(row, TILE), pl.ds(row - 4, TILE))

    def load(kind, p, shift):
        ref = refs[kind]
        first = ref[p, pl.ds(row + shift, TILE), :]
        second = ref[10 + p, pl.ds(row - 4 + shift, TILE), :]
        return jnp.where(upper, first, second)

    def store(p, value):
        new[p, places[0], :] = value
        new[10 + p, places[1], :] = value

    dt = jnp.where(upper, step[places[0], :], step[places[1], :]) * (alpha * 0.2)
    block_update(load, store, jnp.where(upper, coef[50], coef[51]), dt, coef, phase)


def make_moments(cell_ref, weight_ref, count_ref, moments_ref):
    faces = cell_ref.shape[1]
    modes = weight_ref.shape[0]
    cell = cell_ref[...]
    row = lax.shift_right_logical(cell, 7)
    col = jnp.bitwise_and(cell, LANES - 1)
    live = lax.broadcasted_iota(jnp.int32, (1, faces), 1) < count_ref[0]
    weight = jnp.where(live, weight_ref[...], 0.0)
    in_row = lax.broadcasted_iota(jnp.int32, (ROWS, faces), 0) == row
    in_col = (lax.broadcasted_iota(jnp.int32, (LANES, faces), 0) == col).astype(jnp.bfloat16)
    total = None
    for _ in range(3):
        part = weight.astype(jnp.bfloat16)
        weight = weight - part.astype(jnp.float32)
        wide = part.astype(jnp.float32)
        spread = jnp.concatenate(
            [jnp.where(in_row, wide[m : m + 1, :], 0.0) for m in range(modes)], axis=0
        ).astype(jnp.bfloat16)
        term = lax.dot_general(spread, in_col, (((1,), (1,)), ((), ())), preferred_element_type=jnp.float32)
        total = term if total is None else total + term
    moments_ref[...] = total


def make_tables(ids_ref, table_ref):
    blade = lax.broadcasted_iota(jnp.int32, (1, LANES), 1)
    rows = []
    for yl, x in itertools.product(range(SIZES[1]), range(SIZES[0])):
        rows.append(blade * ids_ref[x * SIZES[1] + yl])
    product = jnp.concatenate(rows, axis=0)
    turns = ((product.astype(jnp.float32) + 0.5) * (1.0 / BLADES)).astype(jnp.int32)
    angle = 2.0 * jnp.pi * (product - turns * BLADES).astype(jnp.float32) / BLADES
    n = len(rows)
    table_ref[0:n, :] = jnp.cos(angle)
    table_ref[n : 2 * n, :] = jnp.sin(angle)
    mine = ids_ref[lax.axis_index("x") * SIZES[1] + lax.axis_index("yl")]
    sigma = jnp.full((TILE, LANES), mine, jnp.int32).astype(jnp.float32)
    sigma = 2.0 * jnp.pi * sigma / BLADES
    table_ref[2 * n : 2 * n + 8, :] = jnp.cos(sigma)
    table_ref[2 * n + 8 : 2 * n + 16, :] = jnp.sin(sigma)


def prep_kernel(
    cell_ref, weight_ref, ids_ref, ja_ref, jc_ref, omega_ref, _, count_ref, q_ref, s_ref, t_ref, near_ref,
    moments_ref, table_ref, coef_ref, cell, weight, ids, ja, jc, omega, sems,
):
    pairs = ((cell_ref, cell), (weight_ref, weight), (ids_ref, ids), (ja_ref, ja), (jc_ref, jc), (omega_ref, omega))
    copies = [pltpu.make_async_copy(a, b, sems.at[i]) for i, (a, b) in enumerate(pairs)]
    for copy in copies:
        copy.start()
    last_end = 1 - lax.axis_index("core")
    fill_message(near_ref, last_end * (ROWS - HALO), last_end, q_ref, s_ref, t_ref)
    for copy in copies:
        copy.wait()
    make_coefficients(ja, jc, omega, coef_ref)
    make_tables(ids, table_ref)
    make_moments(cell, weight, count_ref, moments_ref)


def inner_kernel(
    coef, q_ref, s_ref, t_ref, table_ref, rim_ref, core_ref, base, first, second, forced, step,
):
    phase = phases(table_ref)
    own = pl.ds(OWN, ROWS)
    for i in range(PLANES):
        base[i, own, :] = q_ref[i]
        forced[i, own, :] = s_ref[i] * 5.0
    step[own, :] = t_ref[...]

    bufs = (base, first, second, first, base)
    for t in range(1, LEVELS + 1):
        k = (t - 1) % SECTIONS
        cur, new = bufs[k], bufs[k + 1]
        valid = ROWS - 2 * t
        tiles = (valid + TILE - 1) // TILE

        for j in range(tiles):
            tile_update(cur, base, new, forced, step, coef, phase, ALPHAS[k], OWN + t + j * TILE)
        if t < LEVELS:
            for i in range(PLANES):
                rim_ref[t - 1, i, 0:4, :] = new[i, OWN + t : OWN + t + 4, :]
                rim_ref[t - 1, i, 4:8, :] = new[i, OWN + ROWS - 4 - t : OWN + ROWS - t, :]
        else:
            for i in range(PLANES):
                core_ref[i] = new[i, OWN + t : OWN + ROWS - t, :]


def rim_sections(last_end, halo_ref, q_ref, s_ref, t_ref, rim_ref, table_ref, coef, scratch):
    base, other, first, second, forced, step = scratch
    phase = phases(table_ref)
    half = ROWS // 2
    low, mid = TILE, TILE + half
    taken = pl.ds(pl.multiple_of(last_end * half, half), half)
    own = pl.ds(pl.multiple_of(jnp.where(last_end == 1, low, mid), TILE), half)
    halo = pl.ds(jnp.where(last_end == 1, mid, mid - HALO), HALO)
    fewer = pl.ds(jnp.where(last_end == 1, mid, mid - HALO + 1), HALO - 1)
    for i in range(PLANES):
        base[i, own, :] = q_ref[i, taken, :]
        base[i, halo, :] = halo_ref[i * HALO : (i + 1) * HALO, :]
        at = SOURCE_AT + i * (HALO - 1)
        forced[i, own, :] = s_ref[i, taken, :] * 5.0
        forced[i, fewer, :] = halo_ref[at : at + HALO - 1, :] * 5.0
    step[own, :] = t_ref[taken, :]
    step[fewer, :] = halo_ref[STEP_AT : STEP_AT + HALO - 1, :]

    for it in range(ITERS):
        start, end = (base, other) if it % 2 == 0 else (other, base)
        bufs = (start, first, second, first, end)
        for k in range(SECTIONS):
            t = it * SECTIONS + k + 1
            cur, new = bufs[k], bufs[k + 1]
            shared = jnp.where(last_end == 1, mid - t, mid - 4 + t)
            alone = jnp.where(last_end == 1, mid - t + 4, mid - HALO + t)
            mixed_update(cur, start, new, forced, step, coef, phase, ALPHAS[k], shared)
            tile_update(cur, start, new, forced, step, coef, phase, ALPHAS[k], alone)
            if t < LEVELS:
                kept = pl.ds(last_end * 4, 4)
                place = pl.ds(jnp.where(last_end == 1, mid - 4 - t, mid + t), 4)
                for i in range(PLANES):
                    new[i, place, :] = rim_ref[t - 1, i, kept, :]
    return end, jnp.where(last_end == 1, mid - HALO, mid)


def reduce_to_lanes(items):
    sublane = lax.broadcasted_iota(jnp.int32, (TILE, LANES), 0)
    lane = lax.broadcasted_iota(jnp.int32, (TILE, LANES), 1)
    for axis, index, shifts in ((0, sublane, (4, 2, 1)), (1, lane, (64, 32, 16))):
        size = (TILE, LANES)[axis]
        for shift in shifts:
            low = jnp.bitwise_and(index, shift) == 0
            n = len(items) // 2
            items = [
                jnp.where(low, a + pltpu.roll(a, size - shift, axis), b + pltpu.roll(b, shift, axis))
                for a, b in zip(items[:n], items[n:])
            ]
    total = items[0]
    for shift in (8, 4, 2, 1):
        low = jnp.bitwise_and(lane, shift) == 0
        total = total + jnp.where(low, pltpu.roll(total, LANES - shift, 1), pltpu.roll(total, shift, 1))
    kept = jnp.where(jnp.bitwise_and(lane, 15) == sublane, total, 0.0)
    return jnp.sum(kept, axis=0, keepdims=True)


def near_rim_kernel(coef, q_ref, s_ref, t_ref, halo_ref, table_ref, rim_ref, core_ref, half_ref, *scratch):
    last_end = 1 - lax.axis_index("core")
    end, at = rim_sections(last_end, halo_ref, q_ref, s_ref, t_ref, rim_ref, table_ref, coef, scratch)
    fill_half(last_end, end, at, core_ref, half_ref)


def fill_half(last_end, end, at, core_ref, half_ref):
    for i in range(PLANES):
        half_ref[i, pl.ds(last_end * 4, HALO), :] = end[i, pl.ds(at, HALO), :]
        half_ref[i, pl.ds((1 - last_end) * HALO, 4), :] = core_ref[i, pl.ds(last_end * 4, 4), :]


def half_of(ref, last_end):
    half = ROWS // 2
    return ref.at[:, pl.ds(pl.multiple_of(last_end * half, half), half), :]


def far_rim_kernel(
    coef, q_ref, s_ref, t_ref, halo_ref, moments_ref, table_ref, rim_ref, core_ref, near_ref,
    out_ref, half_ref, force_ref, sem, *scratch,
):
    last_end = lax.axis_index("core")
    copy = pltpu.make_async_copy(near_ref, half_of(out_ref, 1 - last_end), sem)
    copy.start()
    end, at = rim_sections(last_end, halo_ref, q_ref, s_ref, t_ref, rim_ref, table_ref, coef, scratch)
    fill_half(last_end, end, at, core_ref, half_ref)

    pressure = []
    for ec in range(4):
        i = ec * 5 + 4
        far = [half_ref[i, r : r + TILE, :] for r in (0, TILE)]
        near = [near_ref[i, r : r + TILE, :] for r in (0, TILE)]
        pressure.append([jnp.where(last_end == 1, n, f) for f, n in zip(far, near)]
                        + [jnp.where(last_end == 1, f, n) for f, n in zip(far, near)])
    items = []
    for at in range(64):
        g, ec, odd = at % 8, at // 8 % 4, at // 32
        m = g // 2 * 4 + g % 2 * 2 + odd
        acc = None
        for r in range(0, ROWS, TILE):
            term = moments_ref[m * ROWS + r : m * ROWS + r + TILE, :] * pressure[ec][r // TILE]
            acc = term if acc is None else acc + term
        items.append(acc)
    force_ref[...] = jnp.broadcast_to(reduce_to_lanes(items), force_ref.shape)
    copy.wait()


def middle_kernel(in_ref, out_ref):
    got = in_ref[...]
    mine = lax.axis_index("yl")
    lane = lax.broadcasted_iota(jnp.int32, (1, LANES), 1)
    keep = lane % 32 < 4
    at = mine // 2 * 16 + mine % 2 * 4
    total = None
    for yl in range(SIZES[1]):
        part = jnp.sum(got[yl * 4 : yl * 4 + 4, :], axis=0, keepdims=True)
        part = pltpu.roll(part, (LANES - at) % LANES, 1)
        part = jnp.where(keep, part, 0.0)
        if yl:
            part = pltpu.roll(part, 4 * yl, 1)
        total = part if total is None else total + part
    out_ref[...] = jnp.broadcast_to(total, out_ref.shape)


def final_kernel(in_ref, table_ref, half_ref, _, out_ref, result_ref, out, sems):
    place = half_of(result_ref, lax.axis_index("core"))
    piece = PLANES // 4
    copies = []
    for i in range(4):
        some = slice(i * piece, (i + 1) * piece)
        copies.append(pltpu.make_async_copy(half_ref.at[some], place.at[some], sems.at[i]))
        copies[i].start()
    mine = lax.axis_index("x")
    depth = SIZES[2]
    parts = [
        jnp.sum(in_ref[x * depth : (x + 1) * depth, :], axis=0, keepdims=True) for x in range(SIZES[0])
    ]
    force = pltpu.roll(jnp.concatenate(parts, axis=0), (LANES - 32 * mine) % LANES, 1)
    n = SIZES[0] * SIZES[1]
    for e in range(2):
        real, imag = None, None
        for yl in range(SIZES[1]):
            at = yl * 4 + e * 2
            f_r = force[:, at : at + 1]
            f_i = force[:, at + 1 : at + 2]
            cosine = table_ref[yl * 4 : yl * 4 + 4, :]
            sine = table_ref[n + yl * 4 : n + yl * 4 + 4, :]
            r = f_r * cosine - f_i * sine
            i = f_r * sine + f_i * cosine
            real = r if real is None else real + r
            imag = i if imag is None else imag + i
        scale = 1.0 / BLADES
        out[0, 0, e : e + 1, :] = (jnp.sum(real, axis=0, keepdims=True) * scale)[:, :BLADES]
        out[0, 1, e : e + 1, :] = (jnp.sum(imag, axis=0, keepdims=True) * scale)[:, :BLADES]
    copies.append(pltpu.make_async_copy(out, out_ref, sems.at[4]))
    copies[4].start()
    for copy in copies:
        copy.wait()


def shape(*dims):
    return jax.ShapeDtypeStruct(dims, jnp.float32)


VMEM = pl.BlockSpec(memory_space=pltpu.VMEM)
SMEM = pl.BlockSpec(memory_space=pltpu.SMEM)
ANY = pl.BlockSpec(memory_space=pltpu.HBM)


def call(kernel, out_shape, in_specs, scratch=(), cost=(1000, 1000), out_specs=None, aliases=()):
    return pl.pallas_call(
        kernel,
        out_shape=out_shape,
        in_specs=in_specs,
        out_specs=out_specs or jax.tree.map(lambda _: VMEM, out_shape),
        scratch_shapes=list(scratch),
        input_output_aliases=dict(aliases),
        compiler_params=pltpu.CompilerParams(vmem_limit_bytes=32 * 1024 * 1024),
        cost_estimate=pl.CostEstimate(flops=cost[0], bytes_accessed=cost[1], transcendentals=0),
    )


def in_hbm(value):
    return pltpu.with_memory_space_constraint(value, pltpu.HBM)


def per_device(
    perturbation, source, time_step, jac_axial, jac_circ, omega, diam_ids, surf_cell, surf_weight, face_count
):
    q = perturbation.reshape(PLANES, ROWS, LANES)
    src = source.reshape(PLANES, ROWS, LANES)
    edge = pltpu.VMEM((PLANES, 16, LANES), jnp.float32)
    far = call(
        far_kernel,
        shape(FAR_MSG, LANES),
        [ANY] * 3,
        [edge, edge, pltpu.VMEM((16, LANES), jnp.float32), pltpu.SemaphoreType.DMA((9,))],
    )(*map(in_hbm, (q, src, time_step)))
    big = pltpu.VMEM((PLANES, ROWS + 16, LANES), jnp.float32)
    faces = surf_cell.shape[0]
    near, moments, table, coef = call(
        prep_kernel,
        (shape(MSG, LANES), shape(16 * ROWS, LANES), shape(48, LANES), shape(52, TILE, LANES)),
        [ANY] * 7 + [SMEM] + [VMEM] * 3,
        [pltpu.VMEM((1, faces), jnp.int32), pltpu.VMEM((16, faces), jnp.float32)]
        + [pltpu.SMEM(diam_ids.shape, jnp.int32), pltpu.VMEM((5, 5), jnp.float32), pltpu.VMEM((5, 5), jnp.float32)]
        + [pltpu.VMEM((1, 2), jnp.float32), pltpu.SemaphoreType.DMA((6,))],
    )(
        *map(in_hbm, (surf_cell.reshape(1, -1), surf_weight, diam_ids, jac_axial, jac_circ, omega.reshape(1, 2))),
        far, face_count, q, src, time_step,
    )
    far = lax.ppermute(far, AXES, swap_pairs(False))
    near = lax.ppermute(near, AXES, swap_pairs(True))
    rim, core = call(
        inner_kernel,
        (shape(LEVELS - 1, PLANES, TILE, LANES), shape(PLANES, TILE, LANES)),
        [VMEM] * 5,
        [big, big, big, big, pltpu.VMEM((ROWS + 16, LANES), jnp.float32)],
    )(coef, q, src, time_step, table)
    big = pltpu.VMEM((PLANES, RIM, LANES), jnp.float32)
    scratch = [big] * 5 + [pltpu.VMEM((RIM, LANES), jnp.float32)]
    half = shape(PLANES, ROWS // 2, LANES)
    near_half = call(near_rim_kernel, half, [VMEM] * 8, scratch)(coef, q, src, time_step, near, table, rim, core)
    result, far_half, force = call(
        far_rim_kernel,
        (shape(PLANES, ROWS, LANES), half, shape(16, LANES)),
        [VMEM] * 10,
        [pltpu.SemaphoreType.DMA] + scratch,
        out_specs=(ANY, VMEM, VMEM),
    )(coef, q, src, time_step, far, moments, table, rim, core, near_half)
    got = lax.all_to_all(force, ("yl", "yh", "core"), 0, 0, tiled=True)
    middle = call(middle_kernel, shape(32, LANES), [VMEM])(got)
    got = lax.all_to_all(middle, ("x", "z"), 0, 0, tiled=True)
    influence, result = call(
        final_kernel,
        (shape(1, 2, 2, BLADES), shape(PLANES, ROWS, LANES)),
        [VMEM] * 3 + [ANY],
        [pltpu.VMEM((1, 2, 2, BLADES), jnp.float32), pltpu.SemaphoreType.DMA((5,))],
        out_specs=(ANY, ANY),
        aliases={3: 1},
    )(got, table, far_half, result)
    return result.reshape(perturbation.shape), influence


def solution(mesh):
    fine = Mesh(mesh.devices.reshape(SIZES), AXES)
    diam, blocks = ("x", "yl"), ("z", "yh", "core")
    in_specs = (
        P(diam, None, None, None, blocks, None),
        P(None, None, None, blocks, None),
        P(blocks, None),
        P(),
        P(),
        P(),
        P(),
        P(blocks),
        P(None, blocks),
        P(blocks),
    )
    out_specs = (P(diam, None, None, None, blocks, None), P(diam, None, None, None))
    return jax.shard_map(per_device, mesh=fine, in_specs=in_specs, out_specs=out_specs, check_vma=False)
```

```python
import itertools

import jax
import jax.numpy as jnp
from jax import lax
from jax.experimental import pallas as pl
from jax.experimental.pallas import tpu as pltpu
from jax.sharding import Mesh
from jax.sharding import PartitionSpec as P

BLADES = 72
ITERS = 3
SECTIONS = 4
HALO = ITERS * SECTIONS
ALPHAS = (0.25, 1.0 / 3.0, 0.5, 1.0)
HIGH = lax.Precision.HIGHEST
AXES = ("x", "yl", "z", "yh", "core")
SIZES = (4, 4, 8, 2, 2)
PLANES = 20
ROWS = 32
LANES = 128
SOURCE_AT = PLANES * HALO
STEP_AT = SOURCE_AT + PLANES * (HALO - 1)
MSG = STEP_AT + HALO
FAR_MSG = MSG + 8
LEVELS = HALO
OWN = 8
RIM = 48
TILE = 8


def flat(*coords):
    out = 0
    for c, n in zip(coords, SIZES):
        out = out * n + c
    return out


def swap_pairs(same_chip):
    pairs = []
    blocks = SIZES[2] * SIZES[3] * SIZES[4]
    for x, yl, p in itertools.product(range(SIZES[0]), range(SIZES[1]), range(blocks)):
        if same_chip:
            q = p ^ 1
        else:
            q = p + 1 if p % 2 else p - 1
        if 0 <= q < blocks:
            ends = [flat(x, yl, b // 4, (b // 2) % 2, b % 2) for b in (p, q)]
            pairs.append(tuple(ends))
    return pairs


def fill_message(out, first, last_end, q_buf, s_buf, t_buf):
    rows = pl.ds(first, HALO)
    fewer = pl.ds(first + last_end, HALO - 1)
    for i in range(PLANES):
        out[i * HALO : (i + 1) * HALO, :] = q_buf[i, rows, :]
        at = SOURCE_AT + i * (HALO - 1)
        out[at : at + HALO - 1, :] = s_buf[i, fewer, :]
    out[STEP_AT : STEP_AT + HALO - 1, :] = t_buf[fewer, :]
    at = MSG - 1
    out[at:, :] = jnp.zeros((out.shape[0] - at, LANES), jnp.float32)


def far_kernel(q_ref, s_ref, t_ref, out_ref, q_buf, s_buf, t_buf, sems):
    core = lax.axis_index("core")
    wide = q_buf.shape[1]
    rows = pl.ds(pl.multiple_of(core * (ROWS - wide), TILE), wide)
    piece = PLANES // 4
    copies = [pltpu.make_async_copy(t_ref.at[rows, :], t_buf, sems.at[8])]
    for i in range(4):
        some = slice(i * piece, (i + 1) * piece)
        copies.append(pltpu.make_async_copy(q_ref.at[some, rows, :], q_buf.at[some], sems.at[i]))
        copies.append(pltpu.make_async_copy(s_ref.at[some, rows, :], s_buf.at[some], sems.at[4 + i]))
    for copy in copies:
        copy.start()
    for copy in copies:
        copy.wait()
    fill_message(out_ref, core * (wide - HALO), core, q_buf, s_buf, t_buf)


def make_coefficients(ja, jc, omega, coef_ref):
    def put(at, value):
        coef_ref[at] = jnp.broadcast_to(value, (TILE, LANES))

    for u in range(5):
        for v in range(5):
            put(u * 5 + v, ja[u : u + 1, v : v + 1] * 2.5)
            put(25 + u * 5 + v, jc[u : u + 1, v : v + 1] * 2.5)
    for e in range(2):
        put(50 + e, omega[:, e : e + 1] * 5.0)


def phases(table_ref):
    lane = lax.broadcasted_iota(jnp.int32, (TILE, LANES), 1)
    is_first, is_last = lane == 0, lane == LANES - 1
    cosine = table_ref[32:40, :]
    sine = table_ref[40:48, :]
    turn_c = jnp.where(is_first | is_last, cosine, 1.0)
    turn_s = jnp.where(is_first, -sine, jnp.where(is_last, sine, 0.0))
    return is_first, is_last, turn_c, turn_s


def block_update(load, store, freq, dt, coef, phase):
    is_first, is_last, turn_c, turn_s = phase
    center = [load("cur", p, 0) for p in range(10)]
    axial, circ, total = [], [], []
    for p in range(10):
        up, down = load("cur", p, 1), load("cur", p, -1)
        mid, other = center[p], center[(p + 5) % 10]
        turned = turn_c * mid + turn_s * other if p < 5 else turn_c * mid - turn_s * other
        right = pltpu.roll(jnp.where(is_first, turned, mid), LANES - 1, 1)
        left = pltpu.roll(jnp.where(is_last, turned, mid), 1, 1)
        axial.append(up - down)
        circ.append(right - left)
        total.append((up + down) + (right + left))
    for p in range(10):
        c, u = divmod(p, 5)
        acc = total[p] + load("forced", p, 0) - 4.0 * center[p]
        spin = freq * center[(p + 5) % 10]
        acc = acc + spin if c == 0 else acc - spin
        conv = None
        for v in range(5):
            a = coef[u * 5 + v] * axial[c * 5 + v]
            b = coef[25 + u * 5 + v] * circ[c * 5 + v]
            conv = a + b if conv is None else conv + (a + b)
        store(p, load("base", p, 0) + dt * (acc - conv))


def tile_update(cur, base, new, forced, step, coef, phase, alpha, row):
    refs = dict(cur=cur, base=base, forced=forced)
    here = pl.ds(row, TILE)
    dt = step[here, :] * (alpha * 0.2)
    for e in range(2):

        def load(kind, p, shift, e=e):
            return refs[kind][e * 10 + p, pl.ds(row + shift, TILE), :]

        def store(p, value, e=e):
            new[e * 10 + p, here, :] = value

        block_update(load, store, coef[50 + e], dt, coef, phase)


def mixed_update(cur, base, new, forced, step, coef, phase, alpha, row):
    refs = dict(cur=cur, base=base, forced=forced)
    upper = lax.broadcasted_iota(jnp.int32, (TILE, LANES), 0) < 4
    places = (pl.ds(row, TILE), pl.ds(row - 4, TILE))

    def load(kind, p, shift):
        ref = refs[kind]
        first = ref[p, pl.ds(row + shift, TILE), :]
        second = ref[10 + p, pl.ds(row - 4 + shift, TILE), :]
        return jnp.where(upper, first, second)

    def store(p, value):
        new[p, places[0], :] = value
        new[10 + p, places[1], :] = value

    dt = jnp.where(upper, step[places[0], :], step[places[1], :]) * (alpha * 0.2)
    block_update(load, store, jnp.where(upper, coef[50], coef[51]), dt, coef, phase)


def make_moments(cell_ref, weight_ref, count_ref, moments_ref):
    faces = cell_ref.shape[1]
    modes = weight_ref.shape[0]
    cell = cell_ref[...]
    row = lax.shift_right_logical(cell, 7)
    col = jnp.bitwise_and(cell, LANES - 1)
    live = lax.broadcasted_iota(jnp.int32, (1, faces), 1) < count_ref[0]
    weight = jnp.where(live, weight_ref[...], 0.0)
    in_row = lax.broadcasted_iota(jnp.int32, (ROWS, faces), 0) == row
    in_col = (lax.broadcasted_iota(jnp.int32, (LANES, faces), 0) == col).astype(jnp.bfloat16)
    total = None
    for _ in range(3):
        part = weight.astype(jnp.bfloat16)
        weight = weight - part.astype(jnp.float32)
        wide = part.astype(jnp.float32)
        spread = jnp.concatenate(
            [jnp.where(in_row, wide[m : m + 1, :], 0.0) for m in range(modes)], axis=0
        ).astype(jnp.bfloat16)
        term = lax.dot_general(spread, in_col, (((1,), (1,)), ((), ())), preferred_element_type=jnp.float32)
        total = term if total is None else total + term
    moments_ref[...] = total


def make_tables(ids_ref, table_ref):
    blade = lax.broadcasted_iota(jnp.int32, (1, LANES), 1)
    rows = []
    for slot in range(SIZES[0] * SIZES[1]):
        rows.append(blade * ids_ref[slot])
    product = jnp.concatenate(rows, axis=0)
    turns = ((product.astype(jnp.float32) + 0.5) * (1.0 / BLADES)).astype(jnp.int32)
    angle = 2.0 * jnp.pi * (product - turns * BLADES).astype(jnp.float32) / BLADES
    n = len(rows)
    table_ref[0:n, :] = jnp.cos(angle)
    table_ref[n : 2 * n, :] = jnp.sin(angle)
    mine = ids_ref[lax.axis_index("x") * SIZES[1] + lax.axis_index("yl")]
    sigma = jnp.full((TILE, LANES), mine, jnp.int32).astype(jnp.float32)
    sigma = 2.0 * jnp.pi * sigma / BLADES
    table_ref[2 * n : 2 * n + 8, :] = jnp.cos(sigma)
    table_ref[2 * n + 8 : 2 * n + 16, :] = jnp.sin(sigma)


def prep_kernel(
    cell_ref, weight_ref, ids_ref, ja_ref, jc_ref, omega_ref, _, count_ref, q_ref, s_ref, t_ref, near_ref,
    moments_ref, table_ref, coef_ref, cell, weight, ids, ja, jc, omega, sems,
):
    pairs = ((cell_ref, cell), (weight_ref, weight), (ids_ref, ids), (ja_ref, ja), (jc_ref, jc), (omega_ref, omega))
    copies = [pltpu.make_async_copy(a, b, sems.at[i]) for i, (a, b) in enumerate(pairs)]
    for copy in copies:
        copy.start()
    last_end = 1 - lax.axis_index("core")
    fill_message(near_ref, last_end * (ROWS - HALO), last_end, q_ref, s_ref, t_ref)
    for copy in copies:
        copy.wait()
    make_coefficients(ja, jc, omega, coef_ref)
    make_tables(ids, table_ref)
    make_moments(cell, weight, count_ref, moments_ref)


def inner_kernel(
    coef, q_ref, s_ref, t_ref, table_ref, rim_ref, core_ref, base, first, second, forced, step,
):
    phase = phases(table_ref)
    own = pl.ds(OWN, ROWS)
    for i in range(PLANES):
        base[i, own, :] = q_ref[i]
        forced[i, own, :] = s_ref[i] * 5.0
    step[own, :] = t_ref[...]

    bufs = (base, first, second, first, base)
    for t in range(1, LEVELS + 1):
        k = (t - 1) % SECTIONS
        cur, new = bufs[k], bufs[k + 1]
        valid = ROWS - 2 * t
        tiles = (valid + TILE - 1) // TILE

        for j in range(tiles):
            tile_update(cur, base, new, forced, step, coef, phase, ALPHAS[k], OWN + t + j * TILE)
        if t < LEVELS:
            for i in range(PLANES):
                rim_ref[t - 1, i, 0:4, :] = new[i, OWN + t : OWN + t + 4, :]
                rim_ref[t - 1, i, 4:8, :] = new[i, OWN + ROWS - 4 - t : OWN + ROWS - t, :]
        else:
            for i in range(PLANES):
                core_ref[i] = new[i, OWN + t : OWN + ROWS - t, :]


def rim_sections(last_end, halo_ref, q_ref, s_ref, t_ref, rim_ref, table_ref, coef, scratch):
    base, other, first, second, forced, step = scratch
    phase = phases(table_ref)
    half = ROWS // 2
    low, mid = TILE, TILE + half
    taken = pl.ds(pl.multiple_of(last_end * half, half), half)
    own = pl.ds(pl.multiple_of(jnp.where(last_end == 1, low, mid), TILE), half)
    halo = pl.ds(jnp.where(last_end == 1, mid, mid - HALO), HALO)
    fewer = pl.ds(jnp.where(last_end == 1, mid, mid - HALO + 1), HALO - 1)
    for i in range(PLANES):
        base[i, own, :] = q_ref[i, taken, :]
        base[i, halo, :] = halo_ref[i * HALO : (i + 1) * HALO, :]
        at = SOURCE_AT + i * (HALO - 1)
        forced[i, own, :] = s_ref[i, taken, :] * 5.0
        forced[i, fewer, :] = halo_ref[at : at + HALO - 1, :] * 5.0
    step[own, :] = t_ref[taken, :]
    step[fewer, :] = halo_ref[STEP_AT : STEP_AT + HALO - 1, :]

    for it in range(ITERS):
        start, end = (base, other) if it % 2 == 0 else (other, base)
        bufs = (start, first, second, first, end)
        for k in range(SECTIONS):
            t = it * SECTIONS + k + 1
            cur, new = bufs[k], bufs[k + 1]
            shared = jnp.where(last_end == 1, mid - t, mid - 4 + t)
            alone = jnp.where(last_end == 1, mid - t + 4, mid - HALO + t)
            mixed_update(cur, start, new, forced, step, coef, phase, ALPHAS[k], shared)
            tile_update(cur, start, new, forced, step, coef, phase, ALPHAS[k], alone)
            if t < LEVELS:
                kept = pl.ds(last_end * 4, 4)
                place = pl.ds(jnp.where(last_end == 1, mid - 4 - t, mid + t), 4)
                for i in range(PLANES):
                    new[i, place, :] = rim_ref[t - 1, i, kept, :]
    return end, jnp.where(last_end == 1, mid - HALO, mid)


def reduce_to_lanes(items):
    sublane = lax.broadcasted_iota(jnp.int32, (TILE, LANES), 0)
    lane = lax.broadcasted_iota(jnp.int32, (TILE, LANES), 1)
    for axis, index, shifts in ((0, sublane, (4, 2, 1)), (1, lane, (64, 32, 16))):
        size = (TILE, LANES)[axis]
        for shift in shifts:
            low = jnp.bitwise_and(index, shift) == 0
            n = len(items) // 2
            items = [
                jnp.where(low, a + pltpu.roll(a, size - shift, axis), b + pltpu.roll(b, shift, axis))
                for a, b in zip(items[:n], items[n:])
            ]
    total = items[0]
    for shift in (8, 4, 2, 1):
        low = jnp.bitwise_and(lane, shift) == 0
        total = total + jnp.where(low, pltpu.roll(total, LANES - shift, 1), pltpu.roll(total, shift, 1))
    kept = jnp.where(jnp.bitwise_and(lane, 15) == sublane, total, 0.0)
    return jnp.sum(kept, axis=0, keepdims=True)


def near_rim_kernel(coef, q_ref, s_ref, t_ref, halo_ref, table_ref, rim_ref, core_ref, half_ref, *scratch):
    last_end = 1 - lax.axis_index("core")
    end, at = rim_sections(last_end, halo_ref, q_ref, s_ref, t_ref, rim_ref, table_ref, coef, scratch)
    fill_half(last_end, end, at, core_ref, half_ref)


def fill_half(last_end, end, at, core_ref, half_ref):
    for i in range(PLANES):
        half_ref[i, pl.ds(last_end * 4, HALO), :] = end[i, pl.ds(at, HALO), :]
        half_ref[i, pl.ds((1 - last_end) * HALO, 4), :] = core_ref[i, pl.ds(last_end * 4, 4), :]


def half_of(ref, last_end):
    half = ROWS // 2
    return ref.at[:, pl.ds(pl.multiple_of(last_end * half, half), half), :]


def far_rim_kernel(
    coef, q_ref, s_ref, t_ref, halo_ref, moments_ref, table_ref, rim_ref, core_ref, near_ref,
    out_ref, half_ref, force_ref, sem, *scratch,
):
    last_end = lax.axis_index("core")
    copy = pltpu.make_async_copy(near_ref, half_of(out_ref, 1 - last_end), sem)
    copy.start()
    end, at = rim_sections(last_end, halo_ref, q_ref, s_ref, t_ref, rim_ref, table_ref, coef, scratch)
    fill_half(last_end, end, at, core_ref, half_ref)

    pressure = []
    for ec in range(4):
        i = ec * 5 + 4
        far = [half_ref[i, r : r + TILE, :] for r in (0, TILE)]
        near = [near_ref[i, r : r + TILE, :] for r in (0, TILE)]
        pressure.append([jnp.where(last_end == 1, n, f) for f, n in zip(far, near)]
                        + [jnp.where(last_end == 1, f, n) for f, n in zip(far, near)])
    items = []
    for at in range(64):
        g, ec, odd = at % 8, at // 8 % 4, at // 32
        m = g // 2 * 4 + g % 2 * 2 + odd
        acc = None
        for r in range(0, ROWS, TILE):
            term = moments_ref[m * ROWS + r : m * ROWS + r + TILE, :] * pressure[ec][r // TILE]
            acc = term if acc is None else acc + term
        items.append(acc)
    force_ref[...] = jnp.broadcast_to(reduce_to_lanes(items), force_ref.shape)
    copy.wait()


def middle_kernel(in_ref, out_ref):
    x, yl = lax.axis_index("x"), lax.axis_index("yl")
    slots = SIZES[0] * SIZES[1]
    rows = [in_ref[2 * n : 2 * n + 1, :] + in_ref[2 * n + 1 : 2 * n + 2, :] for n in range(slots)]
    got = jnp.concatenate(rows, axis=0)
    got = pltpu.roll(got, (LANES - (x * 32 + yl // 2 * 16 + yl % 2 * 4)) % LANES, 1)
    lane = lax.broadcasted_iota(jnp.int32, got.shape, 1)
    got = jnp.where(lane < 4, got, 0.0)
    for shift in (4, 8, 16, 32):
        got = got + pltpu.roll(got, shift, 1)
    kept = jnp.where(lane // 4 == lax.broadcasted_iota(jnp.int32, got.shape, 0), got, 0.0)
    out_ref[...] = jnp.broadcast_to(jnp.sum(kept, axis=0, keepdims=True), out_ref.shape)


def final_kernel(in_ref, table_ref, half_ref, _, out_ref, result_ref, out, sems):
    place = half_of(result_ref, lax.axis_index("core"))
    piece = PLANES // 4
    copies = []
    for i in range(4):
        some = slice(i * piece, (i + 1) * piece)
        copies.append(pltpu.make_async_copy(half_ref.at[some], place.at[some], sems.at[i]))
        copies[i].start()
    n = SIZES[0] * SIZES[1]
    total = jnp.broadcast_to(jnp.sum(in_ref[...], axis=0, keepdims=True), (n, LANES))
    place = lax.broadcasted_iota(jnp.int32, (n, LANES), 1) - 4 * lax.broadcasted_iota(jnp.int32, (n, LANES), 0)
    cosine, sine = table_ref[0:n, :], table_ref[n : 2 * n, :]
    for e in range(2):
        f_r = jnp.sum(jnp.where(place == 2 * e, total, 0.0), axis=1, keepdims=True)
        f_i = jnp.sum(jnp.where(place == 2 * e + 1, total, 0.0), axis=1, keepdims=True)
        real = f_r * cosine - f_i * sine
        imag = f_r * sine + f_i * cosine
        scale = 1.0 / BLADES
        out[0, 0, e : e + 1, :] = (jnp.sum(real, axis=0, keepdims=True) * scale)[:, :BLADES]
        out[0, 1, e : e + 1, :] = (jnp.sum(imag, axis=0, keepdims=True) * scale)[:, :BLADES]
    copies.append(pltpu.make_async_copy(out, out_ref, sems.at[4]))
    copies[4].start()
    for copy in copies:
        copy.wait()


def shape(*dims):
    return jax.ShapeDtypeStruct(dims, jnp.float32)


VMEM = pl.BlockSpec(memory_space=pltpu.VMEM)
SMEM = pl.BlockSpec(memory_space=pltpu.SMEM)
ANY = pl.BlockSpec(memory_space=pltpu.HBM)


def call(kernel, out_shape, in_specs, scratch=(), cost=(1000, 1000), out_specs=None, aliases=()):
    return pl.pallas_call(
        kernel,
        out_shape=out_shape,
        in_specs=in_specs,
        out_specs=out_specs or jax.tree.map(lambda _: VMEM, out_shape),
        scratch_shapes=list(scratch),
        input_output_aliases=dict(aliases),
        compiler_params=pltpu.CompilerParams(vmem_limit_bytes=32 * 1024 * 1024),
        cost_estimate=pl.CostEstimate(flops=cost[0], bytes_accessed=cost[1], transcendentals=0),
    )


def in_hbm(value):
    return pltpu.with_memory_space_constraint(value, pltpu.HBM)


def per_device(
    perturbation, source, time_step, jac_axial, jac_circ, omega, diam_ids, surf_cell, surf_weight, face_count
):
    q = perturbation.reshape(PLANES, ROWS, LANES)
    src = source.reshape(PLANES, ROWS, LANES)
    edge = pltpu.VMEM((PLANES, 16, LANES), jnp.float32)
    far = call(
        far_kernel,
        shape(FAR_MSG, LANES),
        [ANY] * 3,
        [edge, edge, pltpu.VMEM((16, LANES), jnp.float32), pltpu.SemaphoreType.DMA((9,))],
    )(*map(in_hbm, (q, src, time_step)))
    big = pltpu.VMEM((PLANES, ROWS + 16, LANES), jnp.float32)
    faces = surf_cell.shape[0]
    near, moments, table, coef = call(
        prep_kernel,
        (shape(MSG, LANES), shape(16 * ROWS, LANES), shape(48, LANES), shape(52, TILE, LANES)),
        [ANY] * 7 + [SMEM] + [VMEM] * 3,
        [pltpu.VMEM((1, faces), jnp.int32), pltpu.VMEM((16, faces), jnp.float32)]
        + [pltpu.SMEM(diam_ids.shape, jnp.int32), pltpu.VMEM((5, 5), jnp.float32), pltpu.VMEM((5, 5), jnp.float32)]
        + [pltpu.VMEM((1, 2), jnp.float32), pltpu.SemaphoreType.DMA((6,))],
    )(
        *map(in_hbm, (surf_cell.reshape(1, -1), surf_weight, diam_ids, jac_axial, jac_circ, omega.reshape(1, 2))),
        far, face_count, q, src, time_step,
    )
    far = lax.ppermute(far, AXES, swap_pairs(False))
    near = lax.ppermute(near, AXES, swap_pairs(True))
    rim, core = call(
        inner_kernel,
        (shape(LEVELS - 1, PLANES, TILE, LANES), shape(PLANES, TILE, LANES)),
        [VMEM] * 5,
        [big, big, big, big, pltpu.VMEM((ROWS + 16, LANES), jnp.float32)],
    )(coef, q, src, time_step, table)
    big = pltpu.VMEM((PLANES, RIM, LANES), jnp.float32)
    scratch = [big] * 5 + [pltpu.VMEM((RIM, LANES), jnp.float32)]
    half = shape(PLANES, ROWS // 2, LANES)
    near_half = call(near_rim_kernel, half, [VMEM] * 8, scratch)(coef, q, src, time_step, near, table, rim, core)
    result, far_half, force = call(
        far_rim_kernel,
        (shape(PLANES, ROWS, LANES), half, shape(32, LANES)),
        [VMEM] * 10,
        [pltpu.SemaphoreType.DMA] + scratch,
        out_specs=(ANY, VMEM, VMEM),
    )(coef, q, src, time_step, far, moments, table, rim, core, near_half)
    got = lax.all_to_all(force, ("x", "yl", "yh"), 0, 0, tiled=True)
    middle = call(middle_kernel, shape(16, LANES), [VMEM])(got)
    got = lax.all_to_all(middle, ("z", "core"), 0, 0, tiled=True)
    influence, result = call(
        final_kernel,
        (shape(1, 2, 2, BLADES), shape(PLANES, ROWS, LANES)),
        [VMEM] * 3 + [ANY],
        [pltpu.VMEM((1, 2, 2, BLADES), jnp.float32), pltpu.SemaphoreType.DMA((5,))],
        out_specs=(ANY, ANY),
        aliases={3: 1},
    )(got, table, far_half, result)
    return result.reshape(perturbation.shape), influence


def solution(mesh):
    fine = Mesh(mesh.devices.reshape(SIZES), AXES)
    diam, blocks = ("x", "yl"), ("z", "yh", "core")
    in_specs = (
        P(diam, None, None, None, blocks, None),
        P(None, None, None, blocks, None),
        P(blocks, None),
        P(),
        P(),
        P(),
        P(),
        P(blocks),
        P(None, blocks),
        P(blocks),
    )
    out_specs = (P(diam, None, None, None, blocks, None), P(diam, None, None, None))
    return jax.shard_map(per_device, mesh=fine, in_specs=in_specs, out_specs=out_specs, check_vma=False)
```

```python
import itertools

import jax
import jax.numpy as jnp
from jax import lax
from jax.experimental import pallas as pl
from jax.experimental.pallas import tpu as pltpu
from jax.sharding import Mesh
from jax.sharding import PartitionSpec as P

BLADES = 72
ITERS = 3
SECTIONS = 4
HALO = ITERS * SECTIONS
ALPHAS = (0.25, 1.0 / 3.0, 0.5, 1.0)
HIGH = lax.Precision.HIGHEST
AXES = ("x", "yl", "z", "yh", "core")
SIZES = (4, 4, 8, 2, 2)
PLANES = 20
ROWS = 32
LANES = 128
SOURCE_AT = PLANES * HALO
STEP_AT = SOURCE_AT + PLANES * (HALO - 1)
MSG = STEP_AT + HALO
FAR_MSG = MSG + 8
LEVELS = HALO
OWN = 8
RIM = 48
TILE = 8


def flat(*coords):
    out = 0
    for c, n in zip(coords, SIZES):
        out = out * n + c
    return out


def swap_pairs(same_chip):
    pairs = []
    blocks = SIZES[2] * SIZES[3] * SIZES[4]
    for x, yl, p in itertools.product(range(SIZES[0]), range(SIZES[1]), range(blocks)):
        if same_chip:
            q = p ^ 1
        else:
            q = p + 1 if p % 2 else p - 1
        if 0 <= q < blocks:
            ends = [flat(x, yl, b // 4, (b // 2) % 2, b % 2) for b in (p, q)]
            pairs.append(tuple(ends))
    return pairs


def fill_message(out, first, last_end, q_buf, s_buf, t_buf):
    rows = pl.ds(first, HALO)
    fewer = pl.ds(first + last_end, HALO - 1)
    for i in range(PLANES):
        out[i * HALO : (i + 1) * HALO, :] = q_buf[i, rows, :]
        at = SOURCE_AT + i * (HALO - 1)
        out[at : at + HALO - 1, :] = s_buf[i, fewer, :]
    out[STEP_AT : STEP_AT + HALO - 1, :] = t_buf[fewer, :]
    at = MSG - 1
    out[at:, :] = jnp.zeros((out.shape[0] - at, LANES), jnp.float32)


def far_kernel(q_ref, s_ref, t_ref, out_ref, q_buf, s_buf, t_buf, sems):
    core = lax.axis_index("core")
    wide = q_buf.shape[1]
    rows = pl.ds(pl.multiple_of(core * (ROWS - wide), TILE), wide)
    piece = PLANES // 4
    copies = [pltpu.make_async_copy(t_ref.at[rows, :], t_buf, sems.at[8])]
    for i in range(4):
        some = slice(i * piece, (i + 1) * piece)
        copies.append(pltpu.make_async_copy(q_ref.at[some, rows, :], q_buf.at[some], sems.at[i]))
        copies.append(pltpu.make_async_copy(s_ref.at[some, rows, :], s_buf.at[some], sems.at[4 + i]))
    for copy in copies:
        copy.start()
    for copy in copies:
        copy.wait()
    fill_message(out_ref, core * (wide - HALO), core, q_buf, s_buf, t_buf)


def make_coefficients(ja, jc, omega, coef_ref):
    def put(at, value):
        coef_ref[at] = jnp.broadcast_to(value, (TILE, LANES))

    for u in range(5):
        for v in range(5):
            put(u * 5 + v, ja[u : u + 1, v : v + 1] * 2.5)
            put(25 + u * 5 + v, jc[u : u + 1, v : v + 1] * 2.5)
    for e in range(2):
        put(50 + e, omega[:, e : e + 1] * 5.0)


def phases(table_ref):
    lane = lax.broadcasted_iota(jnp.int32, (TILE, LANES), 1)
    is_first, is_last = lane == 0, lane == LANES - 1
    cosine = table_ref[32:40, :]
    sine = table_ref[40:48, :]
    turn_c = jnp.where(is_first | is_last, cosine, 1.0)
    turn_s = jnp.where(is_first, -sine, jnp.where(is_last, sine, 0.0))
    return is_first, is_last, turn_c, turn_s


def block_update(load, store, freq, dt, coef, phase):
    is_first, is_last, turn_c, turn_s = phase
    center = [load("cur", p, 0) for p in range(10)]
    axial, circ, total = [], [], []
    for p in range(10):
        up, down = load("cur", p, 1), load("cur", p, -1)
        mid, other = center[p], center[(p + 5) % 10]
        turned = turn_c * mid + turn_s * other if p < 5 else turn_c * mid - turn_s * other
        right = pltpu.roll(jnp.where(is_first, turned, mid), LANES - 1, 1)
        left = pltpu.roll(jnp.where(is_last, turned, mid), 1, 1)
        axial.append(up - down)
        circ.append(right - left)
        total.append((up + down) + (right + left))
    for p in range(10):
        c, u = divmod(p, 5)
        acc = total[p] + load("forced", p, 0) - 4.0 * center[p]
        spin = freq * center[(p + 5) % 10]
        acc = acc + spin if c == 0 else acc - spin
        conv = None
        for v in range(5):
            a = coef[u * 5 + v] * axial[c * 5 + v]
            b = coef[25 + u * 5 + v] * circ[c * 5 + v]
            conv = a + b if conv is None else conv + (a + b)
        store(p, load("base", p, 0) + dt * (acc - conv))


def tile_update(cur, base, new, forced, step, coef, phase, alpha, row):
    refs = dict(cur=cur, base=base, forced=forced)
    here = pl.ds(row, TILE)
    dt = step[here, :] * (alpha * 0.2)
    for e in range(2):

        def load(kind, p, shift, e=e):
            return refs[kind][e * 10 + p, pl.ds(row + shift, TILE), :]

        def store(p, value, e=e):
            new[e * 10 + p, here, :] = value

        block_update(load, store, coef[50 + e], dt, coef, phase)


def mixed_update(cur, base, new, forced, step, coef, phase, alpha, row):
    refs = dict(cur=cur, base=base, forced=forced)
    upper = lax.broadcasted_iota(jnp.int32, (TILE, LANES), 0) < 4
    places = (pl.ds(row, TILE), pl.ds(row - 4, TILE))

    def load(kind, p, shift):
        ref = refs[kind]
        first = ref[p, pl.ds(row + shift, TILE), :]
        second = ref[10 + p, pl.ds(row - 4 + shift, TILE), :]
        return jnp.where(upper, first, second)

    def store(p, value):
        new[p, places[0], :] = value
        new[10 + p, places[1], :] = value

    dt = jnp.where(upper, step[places[0], :], step[places[1], :]) * (alpha * 0.2)
    block_update(load, store, jnp.where(upper, coef[50], coef[51]), dt, coef, phase)


def make_moments(cell_ref, weight_ref, count_ref, moments_ref):
    faces = cell_ref.shape[1]
    modes = weight_ref.shape[0]
    cell = cell_ref[...]
    row = lax.shift_right_logical(cell, 7)
    col = jnp.bitwise_and(cell, LANES - 1)
    live = lax.broadcasted_iota(jnp.int32, (1, faces), 1) < count_ref[0]
    weight = jnp.where(live, weight_ref[...], 0.0)
    in_row = lax.broadcasted_iota(jnp.int32, (ROWS, faces), 0) == row
    in_col = (lax.broadcasted_iota(jnp.int32, (LANES, faces), 0) == col).astype(jnp.bfloat16)
    total = None
    for _ in range(3):
        part = weight.astype(jnp.bfloat16)
        weight = weight - part.astype(jnp.float32)
        wide = part.astype(jnp.float32)
        spread = jnp.concatenate(
            [jnp.where(in_row, wide[m : m + 1, :], 0.0) for m in range(modes)], axis=0
        ).astype(jnp.bfloat16)
        term = lax.dot_general(spread, in_col, (((1,), (1,)), ((), ())), preferred_element_type=jnp.float32)
        total = term if total is None else total + term
    moments_ref[...] = total


def make_tables(ids_ref, table_ref):
    blade = lax.broadcasted_iota(jnp.int32, (1, LANES), 1)
    rows = []
    for yl, x in itertools.product(range(SIZES[1]), range(SIZES[0])):
        rows.append(blade * ids_ref[x * SIZES[1] + yl])
    product = jnp.concatenate(rows, axis=0)
    turns = ((product.astype(jnp.float32) + 0.5) * (1.0 / BLADES)).astype(jnp.int32)
    angle = 2.0 * jnp.pi * (product - turns * BLADES).astype(jnp.float32) / BLADES
    n = len(rows)
    table_ref[0:n, :] = jnp.cos(angle)
    table_ref[n : 2 * n, :] = jnp.sin(angle)
    mine = ids_ref[lax.axis_index("x") * SIZES[1] + lax.axis_index("yl")]
    sigma = jnp.full((TILE, LANES), mine, jnp.int32).astype(jnp.float32)
    sigma = 2.0 * jnp.pi * sigma / BLADES
    table_ref[2 * n : 2 * n + 8, :] = jnp.cos(sigma)
    table_ref[2 * n + 8 : 2 * n + 16, :] = jnp.sin(sigma)


def prep_kernel(
    cell_ref, weight_ref, ids_ref, ja_ref, jc_ref, omega_ref, q_hbm, s_hbm, t_hbm, _, count_ref, near_ref,
    moments_ref, table_ref, coef_ref, q_ref, s_ref, t_ref, cell, weight, ids, ja, jc, omega, sems,
):
    pairs = ((cell_ref, cell), (weight_ref, weight), (ids_ref, ids), (ja_ref, ja), (jc_ref, jc), (omega_ref, omega))
    pairs += ((q_hbm, q_ref), (s_hbm, s_ref), (t_hbm, t_ref))
    copies = [pltpu.make_async_copy(a, b, sems.at[i]) for i, (a, b) in enumerate(pairs)]
    for copy in copies:
        copy.start()
    last_end = 1 - lax.axis_index("core")
    for copy in copies[:6]:
        copy.wait()
    make_coefficients(ja, jc, omega, coef_ref)
    make_tables(ids, table_ref)
    make_moments(cell, weight, count_ref, moments_ref)
    for copy in copies[6:]:
        copy.wait()
    fill_message(near_ref, last_end * (ROWS - HALO), last_end, q_ref, s_ref, t_ref)


def inner_kernel(
    coef, q_ref, s_ref, t_ref, table_ref, rim_ref, core_ref, base, first, second, forced, step,
):
    phase = phases(table_ref)
    own = pl.ds(OWN, ROWS)
    for i in range(PLANES):
        base[i, own, :] = q_ref[i]
        forced[i, own, :] = s_ref[i] * 5.0
    step[own, :] = t_ref[...]

    bufs = (base, first, second, first, base)
    for t in range(1, LEVELS + 1):
        k = (t - 1) % SECTIONS
        cur, new = bufs[k], bufs[k + 1]
        valid = ROWS - 2 * t
        tiles = (valid + TILE - 1) // TILE

        for j in range(tiles):
            tile_update(cur, base, new, forced, step, coef, phase, ALPHAS[k], OWN + t + j * TILE)
        if t < LEVELS:
            for i in range(PLANES):
                rim_ref[t - 1, i, 0:4, :] = new[i, OWN + t : OWN + t + 4, :]
                rim_ref[t - 1, i, 4:8, :] = new[i, OWN + ROWS - 4 - t : OWN + ROWS - t, :]
        else:
            for i in range(PLANES):
                core_ref[i] = new[i, OWN + t : OWN + ROWS - t, :]


def rim_sections(last_end, halo_ref, q_ref, s_ref, t_ref, rim_ref, table_ref, coef, scratch):
    base, other, first, second, forced, step = scratch
    phase = phases(table_ref)
    half = ROWS // 2
    low, mid = TILE, TILE + half
    taken = pl.ds(pl.multiple_of(last_end * half, half), half)
    own = pl.ds(pl.multiple_of(jnp.where(last_end == 1, low, mid), TILE), half)
    halo = pl.ds(jnp.where(last_end == 1, mid, mid - HALO), HALO)
    fewer = pl.ds(jnp.where(last_end == 1, mid, mid - HALO + 1), HALO - 1)
    for i in range(PLANES):
        base[i, own, :] = q_ref[i, taken, :]
        base[i, halo, :] = halo_ref[i * HALO : (i + 1) * HALO, :]
        at = SOURCE_AT + i * (HALO - 1)
        forced[i, own, :] = s_ref[i, taken, :] * 5.0
        forced[i, fewer, :] = halo_ref[at : at + HALO - 1, :] * 5.0
    step[own, :] = t_ref[taken, :]
    step[fewer, :] = halo_ref[STEP_AT : STEP_AT + HALO - 1, :]

    for it in range(ITERS):
        start, end = (base, other) if it % 2 == 0 else (other, base)
        bufs = (start, first, second, first, end)
        for k in range(SECTIONS):
            t = it * SECTIONS + k + 1
            cur, new = bufs[k], bufs[k + 1]
            shared = jnp.where(last_end == 1, mid - t, mid - 4 + t)
            alone = jnp.where(last_end == 1, mid - t + 4, mid - HALO + t)
            mixed_update(cur, start, new, forced, step, coef, phase, ALPHAS[k], shared)
            tile_update(cur, start, new, forced, step, coef, phase, ALPHAS[k], alone)
            if t < LEVELS:
                kept = pl.ds(last_end * 4, 4)
                place = pl.ds(jnp.where(last_end == 1, mid - 4 - t, mid + t), 4)
                for i in range(PLANES):
                    new[i, place, :] = rim_ref[t - 1, i, kept, :]
    return end, jnp.where(last_end == 1, mid - HALO, mid)


def reduce_to_lanes(items):
    sublane = lax.broadcasted_iota(jnp.int32, (TILE, LANES), 0)
    lane = lax.broadcasted_iota(jnp.int32, (TILE, LANES), 1)
    for axis, index, shifts in ((0, sublane, (4, 2, 1)), (1, lane, (64, 32, 16))):
        size = (TILE, LANES)[axis]
        for shift in shifts:
            low = jnp.bitwise_and(index, shift) == 0
            n = len(items) // 2
            items = [
                jnp.where(low, a + pltpu.roll(a, size - shift, axis), b + pltpu.roll(b, shift, axis))
                for a, b in zip(items[:n], items[n:])
            ]
    total = items[0]
    for shift in (8, 4, 2, 1):
        low = jnp.bitwise_and(lane, shift) == 0
        total = total + jnp.where(low, pltpu.roll(total, LANES - shift, 1), pltpu.roll(total, shift, 1))
    kept = jnp.where(jnp.bitwise_and(lane, 15) == sublane, total, 0.0)
    return jnp.sum(kept, axis=0, keepdims=True)


def near_rim_kernel(coef, q_ref, s_ref, t_ref, halo_ref, table_ref, rim_ref, core_ref, half_ref, *scratch):
    last_end = 1 - lax.axis_index("core")
    end, at = rim_sections(last_end, halo_ref, q_ref, s_ref, t_ref, rim_ref, table_ref, coef, scratch)
    fill_half(last_end, end, at, core_ref, half_ref)


def fill_half(last_end, end, at, core_ref, half_ref):
    for i in range(PLANES):
        half_ref[i, pl.ds(last_end * 4, HALO), :] = end[i, pl.ds(at, HALO), :]
        half_ref[i, pl.ds((1 - last_end) * HALO, 4), :] = core_ref[i, pl.ds(last_end * 4, 4), :]


def half_of(ref, last_end):
    half = ROWS // 2
    return ref.at[:, pl.ds(pl.multiple_of(last_end * half, half), half), :]


def far_rim_kernel(
    coef, q_ref, s_ref, t_ref, halo_ref, moments_ref, table_ref, rim_ref, core_ref, near_ref,
    out_ref, half_ref, force_ref, sem, *scratch,
):
    last_end = lax.axis_index("core")
    copy = pltpu.make_async_copy(near_ref, half_of(out_ref, 1 - last_end), sem)
    copy.start()
    end, at = rim_sections(last_end, halo_ref, q_ref, s_ref, t_ref, rim_ref, table_ref, coef, scratch)
    fill_half(last_end, end, at, core_ref, half_ref)

    pressure = []
    for ec in range(4):
        i = ec * 5 + 4
        far = [half_ref[i, r : r + TILE, :] for r in (0, TILE)]
        near = [near_ref[i, r : r + TILE, :] for r in (0, TILE)]
        pressure.append([jnp.where(last_end == 1, n, f) for f, n in zip(far, near)]
                        + [jnp.where(last_end == 1, f, n) for f, n in zip(far, near)])
    items = []
    for at in range(64):
        g, ec, odd = at % 8, at // 8 % 4, at // 32
        m = g // 2 * 4 + g % 2 * 2 + odd
        acc = None
        for r in range(0, ROWS, TILE):
            term = moments_ref[m * ROWS + r : m * ROWS + r + TILE, :] * pressure[ec][r // TILE]
            acc = term if acc is None else acc + term
        items.append(acc)
    force_ref[...] = jnp.broadcast_to(reduce_to_lanes(items), force_ref.shape)
    copy.wait()


def middle_kernel(in_ref, out_ref):
    got = in_ref[...]
    mine = lax.axis_index("yl")
    lane = lax.broadcasted_iota(jnp.int32, (1, LANES), 1)
    keep = lane % 32 < 4
    at = mine // 2 * 16 + mine % 2 * 4
    total = None
    for yl in range(SIZES[1]):
        part = jnp.sum(got[yl * 4 : yl * 4 + 4, :], axis=0, keepdims=True)
        part = pltpu.roll(part, (LANES - at) % LANES, 1)
        part = jnp.where(keep, part, 0.0)
        if yl:
            part = pltpu.roll(part, 4 * yl, 1)
        total = part if total is None else total + part
    out_ref[...] = jnp.broadcast_to(total, out_ref.shape)


def final_kernel(in_ref, table_ref, half_ref, _, out_ref, result_ref, out, sems):
    place = half_of(result_ref, lax.axis_index("core"))
    piece = PLANES // 4
    copies = []
    for i in range(4):
        some = slice(i * piece, (i + 1) * piece)
        copies.append(pltpu.make_async_copy(half_ref.at[some], place.at[some], sems.at[i]))
        copies[i].start()
    mine = lax.axis_index("x")
    depth = SIZES[2]
    parts = [
        jnp.sum(in_ref[x * depth : (x + 1) * depth, :], axis=0, keepdims=True) for x in range(SIZES[0])
    ]
    force = pltpu.roll(jnp.concatenate(parts, axis=0), (LANES - 32 * mine) % LANES, 1)
    n = SIZES[0] * SIZES[1]
    for e in range(2):
        real, imag = None, None
        for yl in range(SIZES[1]):
            at = yl * 4 + e * 2
            f_r = force[:, at : at + 1]
            f_i = force[:, at + 1 : at + 2]
            cosine = table_ref[yl * 4 : yl * 4 + 4, :]
            sine = table_ref[n + yl * 4 : n + yl * 4 + 4, :]
            r = f_r * cosine - f_i * sine
            i = f_r * sine + f_i * cosine
            real = r if real is None else real + r
            imag = i if imag is None else imag + i
        scale = 1.0 / BLADES
        out[0, 0, e : e + 1, :] = (jnp.sum(real, axis=0, keepdims=True) * scale)[:, :BLADES]
        out[0, 1, e : e + 1, :] = (jnp.sum(imag, axis=0, keepdims=True) * scale)[:, :BLADES]
    copies.append(pltpu.make_async_copy(out, out_ref, sems.at[4]))
    copies[4].start()
    for copy in copies:
        copy.wait()


def shape(*dims):
    return jax.ShapeDtypeStruct(dims, jnp.float32)


VMEM = pl.BlockSpec(memory_space=pltpu.VMEM)
SMEM = pl.BlockSpec(memory_space=pltpu.SMEM)
ANY = pl.BlockSpec(memory_space=pltpu.HBM)


def call(kernel, out_shape, in_specs, scratch=(), cost=(1000, 1000), out_specs=None, aliases=()):
    return pl.pallas_call(
        kernel,
        out_shape=out_shape,
        in_specs=in_specs,
        out_specs=out_specs or jax.tree.map(lambda _: VMEM, out_shape),
        scratch_shapes=list(scratch),
        input_output_aliases=dict(aliases),
        compiler_params=pltpu.CompilerParams(vmem_limit_bytes=32 * 1024 * 1024),
        cost_estimate=pl.CostEstimate(flops=cost[0], bytes_accessed=cost[1], transcendentals=0),
    )


def in_hbm(value):
    return pltpu.with_memory_space_constraint(value, pltpu.HBM)


def per_device(
    perturbation, source, time_step, jac_axial, jac_circ, omega, diam_ids, surf_cell, surf_weight, face_count
):
    q = perturbation.reshape(PLANES, ROWS, LANES)
    src = source.reshape(PLANES, ROWS, LANES)
    edge = pltpu.VMEM((PLANES, 16, LANES), jnp.float32)
    far = call(
        far_kernel,
        shape(FAR_MSG, LANES),
        [ANY] * 3,
        [edge, edge, pltpu.VMEM((16, LANES), jnp.float32), pltpu.SemaphoreType.DMA((9,))],
    )(*map(in_hbm, (q, src, time_step)))
    big = pltpu.VMEM((PLANES, ROWS + 16, LANES), jnp.float32)
    faces = surf_cell.shape[0]
    held = tuple(map(in_hbm, (q, src, time_step)))
    near, moments, table, coef, q, src, time_step = call(
        prep_kernel,
        (
            shape(MSG, LANES), shape(16 * ROWS, LANES), shape(48, LANES), shape(52, TILE, LANES),
            shape(*q.shape), shape(*q.shape), shape(ROWS, LANES),
        ),
        [ANY] * 10 + [SMEM],
        [pltpu.VMEM((1, faces), jnp.int32), pltpu.VMEM((16, faces), jnp.float32)]
        + [pltpu.SMEM(diam_ids.shape, jnp.int32), pltpu.VMEM((5, 5), jnp.float32), pltpu.VMEM((5, 5), jnp.float32)]
        + [pltpu.VMEM((1, 2), jnp.float32), pltpu.SemaphoreType.DMA((9,))],
    )(
        *map(in_hbm, (surf_cell.reshape(1, -1), surf_weight, diam_ids, jac_axial, jac_circ, omega.reshape(1, 2))),
        *held, far, face_count,
    )
    far = lax.ppermute(far, AXES, swap_pairs(False))
    near = lax.ppermute(near, AXES, swap_pairs(True))
    rim, core = call(
        inner_kernel,
        (shape(LEVELS - 1, PLANES, TILE, LANES), shape(PLANES, TILE, LANES)),
        [VMEM] * 5,
        [big, big, big, big, pltpu.VMEM((ROWS + 16, LANES), jnp.float32)],
    )(coef, q, src, time_step, table)
    big = pltpu.VMEM((PLANES, RIM, LANES), jnp.float32)
    scratch = [big] * 5 + [pltpu.VMEM((RIM, LANES), jnp.float32)]
    half = shape(PLANES, ROWS // 2, LANES)
    near_half = call(near_rim_kernel, half, [VMEM] * 8, scratch)(coef, q, src, time_step, near, table, rim, core)
    result, far_half, force = call(
        far_rim_kernel,
        (shape(PLANES, ROWS, LANES), half, shape(16, LANES)),
        [VMEM] * 10,
        [pltpu.SemaphoreType.DMA] + scratch,
        out_specs=(ANY, VMEM, VMEM),
    )(coef, q, src, time_step, far, moments, table, rim, core, near_half)
    got = lax.all_to_all(force, ("yl", "yh", "core"), 0, 0, tiled=True)
    middle = call(middle_kernel, shape(32, LANES), [VMEM])(got)
    got = lax.all_to_all(middle, ("x", "z"), 0, 0, tiled=True)
    influence, result = call(
        final_kernel,
        (shape(1, 2, 2, BLADES), shape(PLANES, ROWS, LANES)),
        [VMEM] * 3 + [ANY],
        [pltpu.VMEM((1, 2, 2, BLADES), jnp.float32), pltpu.SemaphoreType.DMA((5,))],
        out_specs=(ANY, ANY),
        aliases={3: 1},
    )(got, table, far_half, result)
    return result.reshape(perturbation.shape), influence


def solution(mesh):
    fine = Mesh(mesh.devices.reshape(SIZES), AXES)
    diam, blocks = ("x", "yl"), ("z", "yh", "core")
    in_specs = (
        P(diam, None, None, None, blocks, None),
        P(None, None, None, blocks, None),
        P(blocks, None),
        P(),
        P(),
        P(),
        P(),
        P(blocks),
        P(None, blocks),
        P(blocks),
    )
    out_specs = (P(diam, None, None, None, blocks, None), P(diam, None, None, None))
    return jax.shard_map(per_device, mesh=fine, in_specs=in_specs, out_specs=out_specs, check_vma=False)
```
